256 devices in a mesh: tile: 16 (over x, z_hi, core), off: 16 (over z_lo, y).
Axes of the slice: x: 4, y: 4, z: 8 (z_hi: 2, z_lo: 4; z = z_hi * 4 + z_lo), core: 2. Of those that a mesh axis runs over, the one named last changes fastest.
Arguments:
- image_cube: float32 [64, 256, 128, 128], P('off', 'tile'), may hold values from -6 to 6
- time_weight: float32 [256, 128, 128], P('tile'), may hold values from 0.3 to 1
- offset_weight: int32 [64], P('off'), may hold values from 1 to 4
- refine_first: float32 [256, 32], P('tile'), may hold values from -0.375 to 0.375
- refine_second: float32 [128, 16], replicated, may hold values from -0.5 to 0.5
- refine_depth: float32 [128, 16], replicated, may hold values from -0.5 to 0.5
- owner_rows: int32 [32], replicated, may hold values from 0 to 31, each once
Outputs:
- coarse_gradient: float32 [32, 16, 16], P('tile', 'off')
The draws below stay inside these ranges and needn't reach their ends.
Inputs may be any that keep to these rules, and one draw needn't show every extreme that they name: owner_rows names each of the 32 coarse first-dimension indices exactly once.
All inputs are finite; a program needn't handle non-finite values.
Results may differ from the reference program's by a relative error of at most 0.0003.
Values sent between devices are 32-bit elements; how exact they have to be, the bound alone decides.
A program may use at most 64 MiB of HBM per device.

```python
import jax
import jax.numpy as jnp
from jax import lax

NH = 64
NY = 128
NZ = 128
NX = 256
NXC = 32
NYC = 16
NZC = 16


def place_ends(array, own_key, smallest, high):
    dims = array.shape
    place = [jax.random.randint(jax.random.fold_in(own_key, axis), (), 0, dims[axis]) for axis in range(len(dims))]
    array = array.at[tuple(place)].set(smallest)
    longest = dims.index(max(dims))
    place[longest] = (place[longest] + 1) % dims[longest]
    return array.at[tuple(place)].set(high)


def levels(own_key, extent, shards, least, largest):
    def one(dim, blocks):
        heights = jax.random.uniform(jax.random.fold_in(jax.random.fold_in(own_key, 6), dim), (blocks,), jnp.float32, least / len(shards), largest / len(shards))
        return jnp.repeat(jnp.exp(heights), extent[dim] // blocks).reshape((-1,) + (1,) * (len(extent) - dim - 1))

    factor_of = one(*shards[0])
    for cut in shards[1:]:
        factor_of = factor_of * one(*cut)
    return factor_of


def centred(stream_key, dims, spread, limit, cuts=(), kind=jnp.bfloat16):
    array = jax.random.normal(stream_key, dims, jnp.float32) * spread
    if len(cuts) > 0:
        array = levels(stream_key, dims, cuts, -0.22, 0.18) * array
    return jnp.clip(array, min=-limit, max=limit).astype(kind)


def setup_inputs(seed: int = 0) -> dict:
    streams_of = jax.random.split(jax.random.key(seed), 8)
    image_cube = centred(streams_of[0], (NH, NX, NY, NZ), 1.0, 6.0, ((0, 16), (1, 16)), jnp.float32)
    time_weight = jnp.clip(0.3 + 0.7 * jax.random.uniform(streams_of[1], (NX, NY, NZ), jnp.float32) ** levels(streams_of[1], (NX, NY, NZ), ((0, 16),), -0.2, 0.2), 0.3, 1.0)
    offset_weight = place_ends(jax.random.randint(streams_of[2], (NH,), 1, 5), jax.random.fold_in(streams_of[2], 1), 1, 4).astype(jnp.int32)
    refine_first = centred(streams_of[3], (NX, NXC), NX ** -0.5, 0.375, ((0, 16),), jnp.float32)
    refine_second = centred(streams_of[4], (NY, NYC), NY ** -0.5, 0.5, (), jnp.float32)
    refine_depth = centred(streams_of[5], (NZ, NZC), NZ ** -0.5, 0.5, (), jnp.float32)
    owner_rows = jax.random.permutation(streams_of[6], NXC).astype(jnp.int32)
    return dict(image_cube=image_cube, time_weight=time_weight, offset_weight=offset_weight, refine_first=refine_first, refine_second=refine_second, refine_depth=refine_depth, owner_rows=owner_rows)


def fine_gradient(cube, weight_time, offset_scale):
    ahead = jnp.concatenate([cube[1:], jnp.zeros_like(cube[:1])], axis=0)
    difference = ahead - cube
    weights = offset_scale[:, None, None, None] * weight_time[None]
    residual = weights * difference
    weighted = weights * residual
    behind = jnp.concatenate([jnp.zeros_like(weighted[:1]), weighted[:-1]], axis=0)
    adjoint = behind - weighted
    depth_next = jnp.concatenate([cube[..., 1:], jnp.zeros_like(cube[..., :1])], axis=-1)
    depth_diff = depth_next - cube
    return jnp.sum(adjoint * depth_diff, axis=0) / NH


def contract_coarse(fine_grad, rows_first, second, depth):
    highest = lax.Precision.HIGHEST
    along_depth = jnp.einsum("xyz,zc->xyc", fine_grad, depth, precision=highest)
    along_second = jnp.einsum("xyc,yb->xbc", along_depth, second, precision=highest)
    return jnp.einsum("xbc,xa->abc", along_second, rows_first, precision=highest)


def reference(image_cube, time_weight, offset_weight, refine_first, refine_second, refine_depth, owner_rows):
    offset_scale = offset_weight.astype(jnp.float32)
    block_rows = 8
    block_count = NX // block_rows

    def advance(total, index):
        start = (index * block_rows).astype(jnp.int32)
        cube = lax.dynamic_slice_in_dim(image_cube, start, block_rows, 1)
        weight_time = lax.dynamic_slice_in_dim(time_weight, start, block_rows, 0)
        rows_first = lax.dynamic_slice_in_dim(refine_first, start, block_rows, 0)
        fine_grad = fine_gradient(cube, weight_time, offset_scale)
        return total + contract_coarse(fine_grad, rows_first, refine_second, refine_depth), None

    initial = jnp.zeros((NXC, NYC, NZC), jnp.float32)
    coarse, _ = lax.scan(advance, initial, jnp.arange(block_count, dtype=jnp.int32))
    return coarse[owner_rows]
```

```python
import functools

import jax
import jax.numpy as jnp
from jax import lax
from jax.experimental import pallas as pl
from jax.experimental.pallas import tpu as pltpu
from jax.sharding import PartitionSpec as P

MESH = pl.DeviceIdType.MESH
F32 = jnp.float32
BF16 = jnp.bfloat16
HIGHEST = lax.Precision.HIGHEST

NH = 64
LOCAL = 4
ROWS = 16
HALF = 8
N = 128
COARSE = 16
OFFS = 16
TILES = 16


def iota(shape, axis):
    return lax.broadcasted_iota(jnp.int32, shape, axis)


def dot(a, b):
    return jnp.dot(a, b, preferred_element_type=F32)


def split(x):
    high = x.astype(BF16)
    return high, (x - high.astype(F32)).astype(BF16)


def kernel(
    cube, time, weight, first, second, depth, owner, out,
    cube_v, time_v, weight_v, first_v, second_v, depth_v, owner_v,
    before, after, weight_before, grad, place, expand, spread,
    send1, recv1, send2, recv2,
    load_sem, up_send, up_recv, down_send, down_recv, word_send, word_recv,
    s1_send, s1_recv, s2_send, s2_recv,
):
    tile = lax.axis_index("tile")
    off = lax.axis_index("off")
    has_after = off < OFFS - 1
    has_before = off > 0

    barrier = pltpu.get_barrier_semaphore()
    for j in range(1, OFFS):
        pl.semaphore_signal(
            barrier, inc=1, device_id=(tile, lax.rem(off + j, OFFS)), device_id_type=MESH
        )
    for j in range(1, TILES):
        pl.semaphore_signal(
            barrier, inc=1, device_id=(lax.rem(tile + j, TILES), off), device_id_type=MESH
        )
    loads = [
        pltpu.make_async_copy(src, dst, load_sem.at[i])
        for i, (src, dst) in enumerate(
            [
                (weight, weight_v),
                (first, first_v),
                (second, second_v),
                (depth, depth_v),
                (owner, owner_v),
                (time, time_v),
                (cube, cube_v),
            ]
        )
    ]
    for load in loads:
        load.start()
    pl.semaphore_wait(barrier, OFFS - 1 + TILES - 1)

    def up(k):
        return pltpu.make_async_remote_copy(
            src_ref=cube.at[LOCAL - 1, HALF + k],
            dst_ref=before.at[k],
            send_sem=up_send.at[k],
            recv_sem=up_recv.at[k],
            device_id=(tile, off + 1),
            device_id_type=MESH,
        )

    def down(k):
        return pltpu.make_async_remote_copy(
            src_ref=cube.at[0, k],
            dst_ref=after.at[k],
            send_sem=down_send.at[k],
            recv_sem=down_recv.at[k],
            device_id=(tile, off - 1),
            device_id_type=MESH,
        )

    word = pltpu.make_async_remote_copy(
        src_ref=weight,
        dst_ref=weight_before,
        send_sem=word_send,
        recv_sem=word_recv,
        device_id=(tile, off + 1),
        device_id_type=MESH,
    )

    @pl.when(has_after)
    def _():
        word.start()
        for k in range(HALF):
            up(k).start()

    @pl.when(has_before)
    def _():
        for k in range(HALF):
            down(k).start()

    for load in loads:
        load.wait()

    lane = iota((N, N), 1)
    second_high, second_low = split(second_v[...])
    left = jnp.concatenate(
        [
            jnp.concatenate([second_high, second_high], axis=1),
            jnp.concatenate([second_low, jnp.zeros_like(second_low)], axis=1),
        ],
        axis=0,
    )
    depth_wide = jnp.transpose(jnp.concatenate([depth_v[...]] * (N // COARSE), axis=0))
    for q in range(4):
        for p in range(2):
            part = jnp.where(lane // COARSE == 2 * q + p, depth_wide, 0.0)
            high, low = split(part)
            place[q, p * N : (p + 1) * N, :N] = high
            place[q, p * N : (p + 1) * N, N:] = low
    owner_rows = jnp.broadcast_to(owner_v[...].astype(F32), (N, 32))
    for r in range(2):
        pick = (iota((TILES, 32), 1) == 2 * iota((TILES, 32), 0) + r).astype(F32)
        owned = lax.dot_general(
            pick, owner_rows, (((1,), (1,)), ((), ())), precision=HIGHEST,
            preferred_element_type=F32,
        )
        select = (owned[:, :32] == iota((TILES, 32), 1).astype(F32)).astype(F32)
        chosen = lax.dot_general(
            select, first_v[...], (((1,), (1,)), ((), ())), precision=HIGHEST,
            preferred_element_type=F32,
        )
        for h in range(2):
            group = iota((ROWS, N), 1) // COARSE
            row = lax.rem(group, 2) * HALF + h * 4 + group // 2
            where = (row == iota((ROWS, N), 0)).astype(F32)
            expand[r, h] = jnp.dot(chosen, where, precision=HIGHEST, preferred_element_type=F32)
    spread[...] = (
        iota((2 * N, N), 1) == iota((2 * N, N), 0) // N * COARSE + lax.rem(iota((2 * N, N), 0), COARSE)
    ).astype(F32).astype(BF16)

    own = weight_v[...].astype(F32)
    own = own * own
    scale = [
        jnp.sum(jnp.where(iota((1, LOCAL), 1) == h, own, 0.0), axis=1, keepdims=True)
        for h in range(LOCAL)
    ]

    def term(difference, factor):
        last = iota(difference.shape, 1) == N - 1
        following = jnp.where(last, 0.0, pltpu.roll(difference, N - 1, 1))
        return (factor * difference) * (following - difference)

    STEP = 32

    @pl.loop(0, ROWS)
    def _(x):
        for y in range(0, N, STEP):
            rows = pl.ds(y, STEP)
            planes = [cube_v[h, x, rows, :] for h in range(LOCAL)]
            total = term(planes[1] - planes[0], scale[0])
            for h in range(1, LOCAL - 1):
                total += term(planes[h + 1] - planes[h], scale[h])
            grad[x, rows, :] = total
            w = time_v[x, rows, :]
            time_v[x, rows, :] = w * w * (1.0 / NH)

    @pl.when(jnp.logical_not(has_after))
    def _():
        @pl.loop(0, HALF)
        def _(k):
            after[k] = jnp.zeros((N, N), F32)
            for y in range(0, N, STEP):
                rows = pl.ds(y, STEP)
                grad[HALF + k, rows, :] += term(-cube_v[LOCAL - 1, HALF + k, rows, :], scale[3])

    @pl.when(jnp.logical_not(has_before))
    def _():
        weight_before[...] = jnp.zeros((1, LOCAL), jnp.int32)

        @pl.loop(0, HALF)
        def _(k):
            before[k] = jnp.zeros((N, N), F32)

    @pl.when(has_before)
    def _():
        word.wait_recv()

    theirs = weight_before[...].astype(F32)
    theirs = theirs * theirs
    scale_before = jnp.sum(
        jnp.where(iota((1, LOCAL), 1) == LOCAL - 1, theirs, 0.0), axis=1, keepdims=True
    )

    for h in range(2):

        def step(q, coarse, h=h):
            k = h * 4 + q

            @pl.when(has_after)
            def _():
                down(k).wait_recv()

            @pl.when(has_before)
            def _():
                up(k).wait_recv()

            low_rows = time_v[k] * (grad[k] + term(after[k] - cube_v[LOCAL - 1, k], scale[3]))
            high_rows = time_v[HALF + k] * (
                grad[HALF + k] + term(cube_v[0, HALF + k] - before[k], scale_before)
            )
            a_high, a_low = split(low_rows)
            b_high, b_low = split(high_rows)
            right = jnp.concatenate(
                [
                    jnp.concatenate([a_high, b_high], axis=1),
                    jnp.concatenate([a_low, b_low], axis=1),
                ],
                axis=0,
            )
            along = dot(left, right)
            along = along[:COARSE] + along[COARSE:]
            both = dot(jnp.concatenate(split(along), axis=0), place[q])
            return coarse + (
                both[:COARSE, :N] + (both[:COARSE, N:] + both[COARSE:, :N])
            )

        coarse = lax.fori_loop(0, 4, step, jnp.zeros((COARSE, N), F32))
        for b in range(COARSE):
            send1[b, h : h + 1, :] = coarse[b : b + 1]

    def to_off(j):
        peer = lax.rem(off + j, OFFS)
        return pltpu.make_async_remote_copy(
            src_ref=send1.at[peer],
            dst_ref=recv1.at[j],
            send_sem=s1_send,
            recv_sem=s1_recv,
            device_id=(tile, peer),
            device_id_type=MESH,
        )

    for j in range(1, OFFS):
        to_off(j).start()
    recv1[0] = send1[off]
    pltpu.make_async_copy(
        recv1.at[pl.ds(1, OFFS - 1)], recv1.at[pl.ds(1, OFFS - 1)], s1_recv
    ).wait()
    summed = jnp.sum(recv1[...], axis=0)
    lhs = jnp.concatenate(
        [
            expand[r, 0] * summed[0:1, :] + expand[r, 1] * summed[1:2, :]
            for r in range(2)
        ],
        axis=1,
    )
    rows = dot(jnp.concatenate(split(lhs), axis=0), spread[...])
    rows = rows[:TILES] + rows[TILES:]
    for t in range(TILES):
        send2[t, :, :] = rows[t : t + 1]

    def to_tile(j):
        peer = lax.rem(tile + j, TILES)
        return pltpu.make_async_remote_copy(
            src_ref=send2.at[peer],
            dst_ref=recv2.at[j],
            send_sem=s2_send,
            recv_sem=s2_recv,
            device_id=(peer, off),
            device_id_type=MESH,
        )

    for j in range(1, TILES):
        to_tile(j).start()
    recv2[0] = send2[tile]
    pltpu.make_async_copy(
        recv2.at[pl.ds(1, TILES - 1)], recv2.at[pl.ds(1, TILES - 1)], s2_recv
    ).wait()
    result = jnp.sum(recv2[...], axis=0)
    for r in range(2):
        out[r, :, :] = result[:, r * COARSE : (r + 1) * COARSE]

    pltpu.make_async_copy(
        send1.at[pl.ds(0, OFFS - 1)], send1.at[pl.ds(0, OFFS - 1)], s1_send
    ).wait()
    pltpu.make_async_copy(
        send2.at[pl.ds(0, TILES - 1)], send2.at[pl.ds(0, TILES - 1)], s2_send
    ).wait()

    @pl.when(has_after)
    def _():
        word.wait_send()
        for k in range(HALF):
            up(k).wait_send()

    @pl.when(has_before)
    def _():
        for k in range(HALF):
            down(k).wait_send()


def local(cube, time, weight, first, second, depth, owner):
    hbm = pl.BlockSpec(memory_space=pltpu.HBM)
    dma = pltpu.SemaphoreType.DMA
    return pl.pallas_call(
        kernel,
        out_shape=jax.ShapeDtypeStruct((2, 1, COARSE), F32),
        in_specs=[hbm] * 7,
        out_specs=pl.BlockSpec(memory_space=pltpu.VMEM),
        scratch_shapes=[
            pltpu.VMEM((LOCAL, ROWS, N, N), F32),
            pltpu.VMEM((ROWS, N, N), F32),
            pltpu.VMEM((1, LOCAL), jnp.int32),
            pltpu.VMEM((ROWS, 32), F32),
            pltpu.VMEM((COARSE, N), F32),
            pltpu.VMEM((COARSE, N), F32),
            pltpu.VMEM((1, 32), jnp.int32),
            pltpu.VMEM((HALF, N, N), F32),
            pltpu.VMEM((HALF, N, N), F32),
            pltpu.VMEM((1, LOCAL), jnp.int32),
            pltpu.VMEM((ROWS, N, N), F32),
            pltpu.VMEM((4, 2 * N, 2 * N), BF16),
            pltpu.VMEM((2, 2, TILES, N), F32),
            pltpu.VMEM((2 * N, N), BF16),
            pltpu.VMEM((COARSE, 2, N), F32),
            pltpu.VMEM((OFFS, 2, N), F32),
            pltpu.VMEM((TILES, 1, N), F32),
            pltpu.VMEM((TILES, 1, N), F32),
            dma((7,)),
            dma((HALF,)),
            dma((HALF,)),
            dma((HALF,)),
            dma((HALF,)),
            dma,
            dma,
            dma,
            dma,
            dma,
            dma,
        ],
        compiler_params=pltpu.CompilerParams(
            collective_id=0, has_side_effects=True, vmem_limit_bytes=32 * 1024 * 1024
        ),
    )(
        cube,
        time,
        weight.reshape(1, LOCAL),
        first,
        second.T,
        depth.T,
        owner.reshape(1, 32),
    )


def solution(mesh):
    in_specs = (
        P("off", "tile", None, None),
        P("tile", None, None),
        P("off"),
        P("tile", None),
        P(),
        P(),
        P(),
    )
    out_specs = P("tile", "off", None)
    return jax.shard_map(local, mesh=mesh, in_specs=in_specs, out_specs=out_specs, check_vma=False)
```

```python
import jax
import jax.numpy as jnp
from jax import lax
from jax.experimental import pallas as pl
from jax.experimental.pallas import tpu as pltpu
from jax.sharding import PartitionSpec as P

MESH = pl.DeviceIdType.MESH
F32 = jnp.float32
BF16 = jnp.bfloat16
HIGHEST = lax.Precision.HIGHEST

NH = 64
LOCAL = 4
ROWS = 16
HALF = 8
N = 128
COARSE = 16
FIRST = 32
WIDE = FIRST * COARSE
OFFS = 16
GROUP = 16
STRIP = 32


def iota(shape, axis):
    return lax.broadcasted_iota(jnp.int32, shape, axis)


def dot(a, b):
    return jnp.dot(a, b, preferred_element_type=F32)


def split(x):
    high = x.astype(BF16)
    return high, (x - high.astype(F32)).astype(BF16)


def term(difference, factor):
    last = iota(difference.shape, 1) == N - 1
    following = jnp.where(last, 0.0, pltpu.roll(difference, N - 1, 1))
    return (factor * difference) * (following - difference)


def pick(row, index):
    return jnp.sum(jnp.where(iota(row.shape, 1) == index, row, 0.0), axis=1, keepdims=True)


def hops(size, step):
    return min(step, size - step)


PLANE = sorted(
    [(dx, dy) for dx in range(4) for dy in range(4) if dx or dy],
    key=lambda d: (-hops(4, d[0]) - hops(4, d[1]), d),
)
LINE = sorted(
    [(dz, dc) for dz in range(8) for dc in range(2) if dz or dc],
    key=lambda d: (-hops(8, d[0]) - d[1], d),
)


def kernel(
    cube, time, weight, first, second, depth, owner, out,
    cube_v, time_v, weight_v, first_v, second_v, depth_v, owner_v,
    before, after, weight_before, grad, chosen, place,
    send1, recv1, send2, recv2,
    load_sem, up_send, up_recv, down_send, down_recv, word_send, word_recv,
    s1_send, s1_recv, s2_send, s2_recv, near_sem, far_sem, core_sem,
):
    tile = lax.axis_index("tile")
    off = lax.axis_index("off")
    x, z_high, core = lax.div(tile, 4), lax.rem(lax.div(tile, 2), 2), lax.rem(tile, 2)
    z_low, y = lax.div(off, 4), lax.rem(off, 4)
    z = z_high * 4 + z_low
    has_after = off < OFFS - 1
    has_before = off > 0

    def around(dx=0, dy=0, dz=0, dc=0):
        to_x, to_y = lax.rem(x + dx, 4), lax.rem(y + dy, 4)
        to_z, to_core = lax.rem(z + dz, 8), lax.rem(core + dc, 2)
        return (to_x * 4 + lax.div(to_z, 4) * 2 + to_core, lax.rem(to_z, 4) * 4 + to_y)

    def signal(semaphore, device):
        pl.semaphore_signal(semaphore, inc=1, device_id=device, device_id_type=MESH)

    beside = [dict(dy=1), dict(dy=3), dict(dz=1), dict(dz=7), dict(dx=1), dict(dx=3), dict(dc=1)]
    beyond = [dict(dy=2), dict(dz=2), dict(dz=6), dict(dx=2)]
    barrier = pltpu.get_barrier_semaphore()
    turns_after = jnp.logical_and(y == 3, has_after)
    turns_before = jnp.logical_and(y == 0, has_before)

    @pl.when(turns_after)
    def _():
        signal(barrier, (tile, off + 1))

    @pl.when(turns_before)
    def _():
        signal(barrier, (tile, off - 1))

    for d in beside:
        signal(barrier, around(**d))
    loads = [
        pltpu.make_async_copy(src, dst, load_sem.at[i])
        for i, (src, dst) in enumerate(
            [
                (weight, weight_v),
                (first, first_v),
                (second, second_v),
                (depth, depth_v),
                (owner, owner_v),
                (time, time_v),
                (cube, cube_v),
            ]
        )
    ]
    for load in loads[:5]:
        load.start()
    extra = turns_after.astype(jnp.int32) + turns_before.astype(jnp.int32)
    pl.semaphore_wait(barrier, len(beside) + extra)

    def up(k):
        return pltpu.make_async_remote_copy(
            src_ref=cube.at[LOCAL - 1, HALF + k],
            dst_ref=before.at[k],
            send_sem=up_send.at[k],
            recv_sem=up_recv.at[k],
            device_id=(tile, off + 1),
            device_id_type=MESH,
        )

    def down(k):
        return pltpu.make_async_remote_copy(
            src_ref=cube.at[0, k],
            dst_ref=after.at[k],
            send_sem=down_send.at[k],
            recv_sem=down_recv.at[k],
            device_id=(tile, off - 1),
            device_id_type=MESH,
        )

    word = pltpu.make_async_remote_copy(
        src_ref=weight,
        dst_ref=weight_before,
        send_sem=word_send,
        recv_sem=word_recv,
        device_id=(tile, off + 1),
        device_id_type=MESH,
    )

    @pl.when(has_after)
    def _():
        word.start()
        for k in range(HALF):
            up(k).start()

    @pl.when(has_before)
    def _():
        for k in range(HALF):
            down(k).start()

    for d in beside:
        signal(near_sem, around(**d))
    for load in loads[5:]:
        load.start()
    for load in loads[:5]:
        load.wait()

    rows = [second_v[b : b + 1, :] for q in range(4) for b in range(q, COARSE, 4)]
    second_high, second_low = split(jnp.concatenate(rows, axis=0))
    left = jnp.concatenate(
        [
            jnp.concatenate([second_high, second_high], axis=1),
            jnp.concatenate([second_low, jnp.zeros_like(second_low)], axis=1),
        ],
        axis=0,
    )

    unit = (iota((FIRST, WIDE), 0) == iota((FIRST, WIDE), 1) // COARSE).astype(F32)
    owners = jnp.dot(
        jnp.broadcast_to(owner_v[...].astype(F32), (8, FIRST)), unit,
        precision=HIGHEST, preferred_element_type=F32,
    )
    owned = (iota((FIRST, WIDE), 0).astype(F32) == owners[0:1]).astype(F32)
    chosen[...] = jnp.dot(first_v[...], owned, precision=HIGHEST, preferred_element_type=F32)
    depth_wide = jnp.transpose(jnp.concatenate([depth_v[...]] * (N // COARSE), axis=0))

    @pl.loop(0, HALF)
    def _(k):
        for p in range(2):
            row = chosen[pl.ds(p * HALF + k, 1), :]
            for g in range(WIDE // N):
                high, low = split(depth_wide * row[:, g * N : (g + 1) * N])
                place[k, p * N : (p + 1) * N, g * N : (g + 1) * N] = high
                place[k, p * N : (p + 1) * N, WIDE + g * N : WIDE + (g + 1) * N] = low

    pl.semaphore_wait(near_sem, len(beside))
    for d in beyond:
        signal(far_sem, around(**d))

    own = weight_v[...].astype(F32)
    scale = [pick(own * own, h) for h in range(LOCAL)]

    for load in loads[5:]:
        load.wait()

    @pl.loop(0, ROWS)
    def _(r):
        for s in range(0, N, STRIP):
            strip = pl.ds(s, STRIP)
            planes = [cube_v[h, r, strip, :] for h in range(LOCAL)]
            total = term(planes[1] - planes[0], scale[0])
            for h in range(1, LOCAL - 1):
                total += term(planes[h + 1] - planes[h], scale[h])
            grad[r, strip, :] = total
            w = time_v[r, strip, :]
            time_v[r, strip, :] = w * w * (1.0 / NH)

    pl.semaphore_wait(far_sem, len(beyond))
    signal(core_sem, around(dc=1))

    @pl.when(jnp.logical_not(has_after))
    def _():
        @pl.loop(0, HALF)
        def _(k):
            after[k] = jnp.zeros((N, N), F32)
            for s in range(0, N, STRIP):
                strip = pl.ds(s, STRIP)
                grad[HALF + k, strip, :] += term(
                    -cube_v[LOCAL - 1, HALF + k, strip, :], scale[LOCAL - 1]
                )

    @pl.when(jnp.logical_not(has_before))
    def _():
        weight_before[...] = jnp.zeros((1, LOCAL), jnp.int32)

        @pl.loop(0, HALF)
        def _(k):
            before[k] = jnp.zeros((N, N), F32)

    @pl.when(has_before)
    def _():
        word.wait_recv()

    theirs = weight_before[...].astype(F32)
    scale_before = pick(theirs * theirs, LOCAL - 1)

    def step(k, coarse):
        @pl.when(has_after)
        def _():
            down(k).wait_recv()

        @pl.when(has_before)
        def _():
            up(k).wait_recv()

        low_rows = time_v[k] * (grad[k] + term(after[k] - cube_v[LOCAL - 1, k], scale[LOCAL - 1]))
        high_rows = time_v[HALF + k] * (
            grad[HALF + k] + term(cube_v[0, HALF + k] - before[k], scale_before)
        )
        a_high, a_low = split(low_rows)
        b_high, b_low = split(high_rows)
        right = jnp.concatenate(
            [
                jnp.concatenate([a_high, b_high], axis=1),
                jnp.concatenate([a_low, b_low], axis=1),
            ],
            axis=0,
        )
        along = dot(left, right)
        along = along[:COARSE] + along[COARSE:]
        both = dot(jnp.concatenate(split(along), axis=0), place[k])
        both = both[:COARSE] + both[COARSE:]
        return coarse + (both[:, :WIDE] + both[:, WIDE:])

    pl.semaphore_wait(core_sem, 1)
    coarse = lax.fori_loop(0, HALF, step, jnp.zeros((COARSE, WIDE), F32))
    for to_x in range(4):
        for to_y in range(4):
            send1[to_x * 4 + to_y] = coarse[to_y * 4 : to_y * 4 + 4, to_x * N : (to_x + 1) * N]

    def to_plane(dx, dy):
        index = lax.rem(x + dx, 4) * 4 + lax.rem(y + dy, 4)
        return pltpu.make_async_remote_copy(
            src_ref=send1.at[index],
            dst_ref=recv1.at[dx * 4 + dy],
            send_sem=s1_send,
            recv_sem=s1_recv,
            device_id=around(dx=dx, dy=dy),
            device_id_type=MESH,
        )

    for d in PLANE:
        to_plane(*d).start()
    recv1[0] = send1[x * 4 + y]
    landed = recv1.at[pl.ds(1, GROUP - 1)]
    pltpu.make_async_copy(landed, landed, s1_recv).wait()
    summed = jnp.sum(recv1[...], axis=0)
    for q in range(4):
        send2[q] = summed[q : q + 1]

    def to_line(dz, dc):
        index = lax.rem(z + dz, 4)
        return pltpu.make_async_remote_copy(
            src_ref=send2.at[index],
            dst_ref=recv2.at[dz * 2 + dc],
            send_sem=s2_send,
            recv_sem=s2_recv,
            device_id=around(dz=dz, dc=dc),
            device_id_type=MESH,
        )

    for d in LINE:
        to_line(*d).start()
    recv2[0] = send2[z_low]
    landed = recv2.at[pl.ds(1, GROUP - 1)]
    pltpu.make_async_copy(landed, landed, s2_recv).wait()
    result = jnp.sum(recv2[...], axis=0)
    mine = z_high * 2 + core
    result = pltpu.roll(result, lax.rem(4 - mine, 4) * (2 * COARSE), 1)
    for r in range(2):
        out[r] = result[:, r * COARSE : (r + 1) * COARSE]

    left1 = send1.at[pl.ds(0, GROUP - 1)]
    pltpu.make_async_copy(left1, left1, s1_send).wait()
    left2 = recv2.at[pl.ds(0, GROUP - 1)]
    pltpu.make_async_copy(left2, left2, s2_send).wait()

    @pl.when(has_after)
    def _():
        word.wait_send()
        for k in range(HALF):
            up(k).wait_send()

    @pl.when(has_before)
    def _():
        for k in range(HALF):
            down(k).wait_send()


def local(cube, time, weight, first, second, depth, owner):
    hbm = pl.BlockSpec(memory_space=pltpu.HBM)
    dma = pltpu.SemaphoreType.DMA
    return pl.pallas_call(
        kernel,
        out_shape=jax.ShapeDtypeStruct((2, 1, COARSE), F32),
        in_specs=[hbm] * 7,
        out_specs=pl.BlockSpec(memory_space=pltpu.VMEM),
        scratch_shapes=[
            pltpu.VMEM((LOCAL, ROWS, N, N), F32),
            pltpu.VMEM((ROWS, N, N), F32),
            pltpu.VMEM((1, LOCAL), jnp.int32),
            pltpu.VMEM((ROWS, FIRST), F32),
            pltpu.VMEM((COARSE, N), F32),
            pltpu.VMEM((COARSE, N), F32),
            pltpu.VMEM((1, FIRST), jnp.int32),
            pltpu.VMEM((HALF, N, N), F32),
            pltpu.VMEM((HALF, N, N), F32),
            pltpu.VMEM((1, LOCAL), jnp.int32),
            pltpu.VMEM((ROWS, N, N), F32),
            pltpu.VMEM((ROWS, WIDE), F32),
            pltpu.VMEM((HALF, 2 * N, 2 * WIDE), BF16),
            pltpu.VMEM((GROUP, 4, N), F32),
            pltpu.VMEM((GROUP, 4, N), F32),
            pltpu.VMEM((4, 1, N), F32),
            pltpu.VMEM((GROUP, 1, N), F32),
            dma((7,)),
            dma((HALF,)),
            dma((HALF,)),
            dma((HALF,)),
            dma((HALF,)),
            dma,
            dma,
            dma,
            dma,
            dma,
            dma,
            pltpu.SemaphoreType.REGULAR,
            pltpu.SemaphoreType.REGULAR,
            pltpu.SemaphoreType.REGULAR,
        ],
        compiler_params=pltpu.CompilerParams(
            collective_id=0, has_side_effects=True, vmem_limit_bytes=60 * 1024 * 1024
        ),
    )(
        cube,
        time,
        weight.reshape(1, LOCAL),
        first,
        second.T,
        depth.T,
        owner.reshape(1, FIRST),
    )


def solution(mesh):
    in_specs = (
        P("off", "tile", None, None),
        P("tile", None, None),
        P("off"),
        P("tile", None),
        P(),
        P(),
        P(),
    )
    out_specs = P("tile", "off", None)
    return jax.shard_map(local, mesh=mesh, in_specs=in_specs, out_specs=out_specs, check_vma=False)
```

```python
import jax
import jax.numpy as jnp
from jax import lax
from jax.experimental import pallas as pl
from jax.experimental.pallas import tpu as pltpu
from jax.sharding import PartitionSpec as P

MESH = pl.DeviceIdType.MESH
F32 = jnp.float32
BF16 = jnp.bfloat16
HIGHEST = lax.Precision.HIGHEST

NH = 64
LOCAL = 4
ROWS = 16
HALF = 8
N = 128
COARSE = 16
FIRST = 32
WIDE = FIRST * COARSE
OFFS = 16
GROUP = 16
STRIP = 32
PARTS = [(0, 4), (4, 2), (6, 1), (7, 1)]


def iota(shape, axis):
    return lax.broadcasted_iota(jnp.int32, shape, axis)


def dot(a, b):
    return jnp.dot(a, b, preferred_element_type=F32)


def split(x):
    high = x.astype(BF16)
    return high, (x - high.astype(F32)).astype(BF16)


def term(difference, factor):
    last = iota(difference.shape, 1) == N - 1
    following = jnp.where(last, 0.0, pltpu.roll(difference, N - 1, 1))
    return (factor * difference) * (following - difference)


def pick(row, index):
    return jnp.sum(jnp.where(iota(row.shape, 1) == index, row, 0.0), axis=1, keepdims=True)


def hops(size, step):
    return min(step, size - step)


PLANE = sorted(
    [(dx, dy) for dx in range(4) for dy in range(4) if dx or dy],
    key=lambda d: (-hops(4, d[0]) - hops(4, d[1]), d),
)
LINE = sorted(
    [(dz, dc) for dz in range(8) for dc in range(2) if dz or dc],
    key=lambda d: (-hops(8, d[0]) - d[1], d),
)


def kernel(
    cube, time, weight, first, second, depth, owner, out,
    cube_v, time_v, weight_v, first_v, second_v, depth_v, owner_v,
    before, after, weight_before, grad, chosen, place,
    send1, recv1, send2, recv2,
    load_sem, up_send, up_recv, down_send, down_recv, word_send, word_recv,
    s1_send, s1_recv, s2_send, s2_recv, near_sem, far_sem, core_sem,
):
    tile = lax.axis_index("tile")
    off = lax.axis_index("off")
    x, z_high, core = lax.div(tile, 4), lax.rem(lax.div(tile, 2), 2), lax.rem(tile, 2)
    z_low, y = lax.div(off, 4), lax.rem(off, 4)
    z = z_high * 4 + z_low
    has_after = off < OFFS - 1
    has_before = off > 0

    tile_x = [lax.rem(x + dx, 4) * 4 for dx in range(4)]
    off_y = [lax.rem(y + dy, 4) for dy in range(4)]
    cores = [core, 1 - core]
    turned = [lax.rem(z + dz, 8) for dz in range(8)]
    tile_z = [lax.div(to_z, 4) * 2 for to_z in turned]
    row_z = [lax.rem(to_z, 4) for to_z in turned]
    rest_tile, rest_off = z_high * 2 + core, z_low * 4
    plane_tile = [tile_x[dx] + rest_tile for dx in range(4)]
    plane_off = [rest_off + off_y[dy] for dy in range(4)]
    line_tile = [[tile_x[0] + tile_z[dz] + cores[dc] for dc in range(2)] for dz in range(8)]
    line_off = [row_z[dz] * 4 + y for dz in range(8)]

    def around(dx=0, dy=0, dz=0, dc=0):
        if dx or dy:
            return plane_tile[dx], plane_off[dy]
        return line_tile[dz][dc], line_off[dz]

    def signal(semaphore, device):
        pl.semaphore_signal(semaphore, inc=1, device_id=device, device_id_type=MESH)

    beside = [dict(dy=1), dict(dy=3), dict(dz=1), dict(dz=7), dict(dx=1), dict(dx=3), dict(dc=1)]
    beyond = [dict(dy=2), dict(dz=2), dict(dz=6), dict(dx=2)]
    barrier = pltpu.get_barrier_semaphore()
    turns_after = jnp.logical_and(y == 3, has_after)
    turns_before = jnp.logical_and(y == 0, has_before)

    @pl.when(turns_after)
    def _():
        signal(barrier, (tile, off + 1))

    @pl.when(turns_before)
    def _():
        signal(barrier, (tile, off - 1))

    for d in beside:
        signal(barrier, around(**d))
    loads = [
        pltpu.make_async_copy(src, dst, load_sem.at[i])
        for i, (src, dst) in enumerate(
            [
                (weight, weight_v),
                (first, first_v),
                (second, second_v),
                (depth, depth_v),
                (owner, owner_v),
                (time, time_v),
                (cube, cube_v),
            ]
        )
    ]
    extra = turns_after.astype(jnp.int32) + turns_before.astype(jnp.int32)
    pl.semaphore_wait(barrier, len(beside) + extra)

    def up(k):
        start, size = PARTS[k]
        return pltpu.make_async_remote_copy(
            src_ref=cube.at[LOCAL - 1, pl.ds(HALF + start, size)],
            dst_ref=before.at[pl.ds(start, size)],
            send_sem=up_send.at[k],
            recv_sem=up_recv.at[k],
            device_id=(tile, off + 1),
            device_id_type=MESH,
        )

    def down(k):
        start, size = PARTS[k]
        return pltpu.make_async_remote_copy(
            src_ref=cube.at[0, pl.ds(start, size)],
            dst_ref=after.at[pl.ds(start, size)],
            send_sem=down_send.at[k],
            recv_sem=down_recv.at[k],
            device_id=(tile, off - 1),
            device_id_type=MESH,
        )

    word = pltpu.make_async_remote_copy(
        src_ref=weight,
        dst_ref=weight_before,
        send_sem=word_send,
        recv_sem=word_recv,
        device_id=(tile, off + 1),
        device_id_type=MESH,
    )

    @pl.when(has_after)
    def _():
        word.start()
        for k in range(len(PARTS)):
            up(k).start()

    @pl.when(has_before)
    def _():
        for k in range(len(PARTS)):
            down(k).start()

    for d in beside:
        signal(near_sem, around(**d))
    for load in loads:
        load.start()
    for load in loads[:5]:
        load.wait()

    rows = [second_v[b : b + 1, :] for q in range(4) for b in range(q, COARSE, 4)]
    second_high, second_low = split(jnp.concatenate(rows, axis=0))
    left = jnp.concatenate(
        [
            jnp.concatenate([second_high, second_high], axis=1),
            jnp.concatenate([second_low, jnp.zeros_like(second_low)], axis=1),
        ],
        axis=0,
    )

    unit = (iota((FIRST, WIDE), 0) == iota((FIRST, WIDE), 1) // COARSE).astype(F32)
    owners = jnp.dot(
        jnp.broadcast_to(owner_v[...].astype(F32), (8, FIRST)), unit,
        precision=HIGHEST, preferred_element_type=F32,
    )
    owned = (iota((FIRST, WIDE), 0).astype(F32) == owners[0:1]).astype(F32)
    chosen[...] = jnp.dot(first_v[...], owned, precision=HIGHEST, preferred_element_type=F32)
    depth_wide = jnp.transpose(jnp.concatenate([depth_v[...]] * (N // COARSE), axis=0))

    @pl.loop(0, HALF)
    def _(k):
        for p in range(2):
            row = chosen[pl.ds(p * HALF + k, 1), :]
            for g in range(WIDE // N):
                high, low = split(depth_wide * row[:, g * N : (g + 1) * N])
                place[k, p * N : (p + 1) * N, g * N : (g + 1) * N] = high
                place[k, p * N : (p + 1) * N, WIDE + g * N : WIDE + (g + 1) * N] = low

    pl.semaphore_wait(near_sem, len(beside))
    for d in beyond:
        signal(far_sem, around(**d))

    own = weight_v[...].astype(F32)
    scale = [pick(own * own, h) for h in range(LOCAL)]

    for load in loads[5:]:
        load.wait()

    @pl.loop(0, ROWS)
    def _(r):
        for s in range(0, N, STRIP):
            strip = pl.ds(s, STRIP)
            planes = [cube_v[h, r, strip, :] for h in range(LOCAL)]
            total = term(planes[1] - planes[0], scale[0])
            for h in range(1, LOCAL - 1):
                total += term(planes[h + 1] - planes[h], scale[h])
            grad[r, strip, :] = total
            w = time_v[r, strip, :]
            time_v[r, strip, :] = w * w * (1.0 / NH)

    pl.semaphore_wait(far_sem, len(beyond))
    signal(core_sem, around(dc=1))

    @pl.when(jnp.logical_not(has_after))
    def _():
        @pl.loop(0, HALF)
        def _(k):
            after[k] = jnp.zeros((N, N), F32)
            for s in range(0, N, STRIP):
                strip = pl.ds(s, STRIP)
                grad[HALF + k, strip, :] += term(
                    -cube_v[LOCAL - 1, HALF + k, strip, :], scale[LOCAL - 1]
                )

    @pl.when(jnp.logical_not(has_before))
    def _():
        weight_before[...] = jnp.zeros((1, LOCAL), jnp.int32)

        @pl.loop(0, HALF)
        def _(k):
            before[k] = jnp.zeros((N, N), F32)

    @pl.when(has_before)
    def _():
        word.wait_recv()

    theirs = weight_before[...].astype(F32)
    scale_before = pick(theirs * theirs, LOCAL - 1)

    def step(k, coarse):
        low_rows = time_v[k] * (grad[k] + term(after[k] - cube_v[LOCAL - 1, k], scale[LOCAL - 1]))
        high_rows = time_v[HALF + k] * (
            grad[HALF + k] + term(cube_v[0, HALF + k] - before[k], scale_before)
        )
        a_high, a_low = split(low_rows)
        b_high, b_low = split(high_rows)
        right = jnp.concatenate(
            [
                jnp.concatenate([a_high, b_high], axis=1),
                jnp.concatenate([a_low, b_low], axis=1),
            ],
            axis=0,
        )
        along = dot(left, right)
        along = along[:COARSE] + along[COARSE:]
        both = dot(jnp.concatenate(split(along), axis=0), place[k])
        both = both[:COARSE] + both[COARSE:]
        return coarse + (both[:, :WIDE] + both[:, WIDE:])

    pl.semaphore_wait(core_sem, 1)
    coarse = jnp.zeros((COARSE, WIDE), F32)
    for k, (start, size) in enumerate(PARTS):

        @pl.when(has_after)
        def _():
            down(k).wait_recv()

        @pl.when(has_before)
        def _():
            up(k).wait_recv()

        if size > 1:
            coarse = lax.fori_loop(start, start + size, step, coarse)
        else:
            coarse = step(start, coarse)
    for to_x in range(4):
        for to_y in range(4):
            send1[to_x * 4 + to_y] = coarse[to_y * 4 : to_y * 4 + 4, to_x * N : (to_x + 1) * N]

    def to_plane(dx, dy):
        index = tile_x[dx] + off_y[dy]
        return pltpu.make_async_remote_copy(
            src_ref=send1.at[index],
            dst_ref=recv1.at[dx * 4 + dy],
            send_sem=s1_send,
            recv_sem=s1_recv,
            device_id=around(dx=dx, dy=dy),
            device_id_type=MESH,
        )

    for d in PLANE:
        to_plane(*d).start()
    recv1[0] = send1[x * 4 + y]
    landed = recv1.at[pl.ds(1, GROUP - 1)]
    pltpu.make_async_copy(landed, landed, s1_recv).wait()
    summed = jnp.sum(recv1[...], axis=0)
    for q in range(4):
        send2[q] = summed[q : q + 1]

    def to_line(dz, dc):
        index = row_z[dz]
        return pltpu.make_async_remote_copy(
            src_ref=send2.at[index],
            dst_ref=recv2.at[dz * 2 + dc],
            send_sem=s2_send,
            recv_sem=s2_recv,
            device_id=around(dz=dz, dc=dc),
            device_id_type=MESH,
        )

    for d in LINE:
        to_line(*d).start()
    recv2[0] = send2[z_low]
    landed = recv2.at[pl.ds(1, GROUP - 1)]
    pltpu.make_async_copy(landed, landed, s2_recv).wait()
    result = jnp.sum(recv2[...], axis=0)
    mine = z_high * 2 + core
    result = pltpu.roll(result, lax.rem(4 - mine, 4) * (2 * COARSE), 1)
    for r in range(2):
        out[r] = result[:, r * COARSE : (r + 1) * COARSE]

    left1 = send1.at[pl.ds(0, GROUP - 1)]
    pltpu.make_async_copy(left1, left1, s1_send).wait()
    left2 = recv2.at[pl.ds(0, GROUP - 1)]
    pltpu.make_async_copy(left2, left2, s2_send).wait()

    @pl.when(has_after)
    def _():
        word.wait_send()
        for k in range(len(PARTS)):
            up(k).wait_send()

    @pl.when(has_before)
    def _():
        for k in range(len(PARTS)):
            down(k).wait_send()


def local(cube, time, weight, first, second, depth, owner):
    hbm = pl.BlockSpec(memory_space=pltpu.HBM)
    dma = pltpu.SemaphoreType.DMA
    return pl.pallas_call(
        kernel,
        out_shape=jax.ShapeDtypeStruct((2, 1, COARSE), F32),
        in_specs=[hbm] * 7,
        out_specs=pl.BlockSpec(memory_space=pltpu.VMEM),
        scratch_shapes=[
            pltpu.VMEM((LOCAL, ROWS, N, N), F32),
            pltpu.VMEM((ROWS, N, N), F32),
            pltpu.VMEM((1, LOCAL), jnp.int32),
            pltpu.VMEM((ROWS, FIRST), F32),
            pltpu.VMEM((COARSE, N), F32),
            pltpu.VMEM((COARSE, N), F32),
            pltpu.VMEM((1, FIRST), jnp.int32),
            pltpu.VMEM((HALF, N, N), F32),
            pltpu.VMEM((HALF, N, N), F32),
            pltpu.VMEM((1, LOCAL), jnp.int32),
            pltpu.VMEM((ROWS, N, N), F32),
            pltpu.VMEM((ROWS, WIDE), F32),
            pltpu.VMEM((HALF, 2 * N, 2 * WIDE), BF16),
            pltpu.VMEM((GROUP, 4, N), F32),
            pltpu.VMEM((GROUP, 4, N), F32),
            pltpu.VMEM((4, 1, N), F32),
            pltpu.VMEM((GROUP, 1, N), F32),
            dma((7,)),
            dma((len(PARTS),)),
            dma((len(PARTS),)),
            dma((len(PARTS),)),
            dma((len(PARTS),)),
            dma,
            dma,
            dma,
            dma,
            dma,
            dma,
            pltpu.SemaphoreType.REGULAR,
            pltpu.SemaphoreType.REGULAR,
            pltpu.SemaphoreType.REGULAR,
        ],
        compiler_params=pltpu.CompilerParams(
            collective_id=0, has_side_effects=True, vmem_limit_bytes=24 * 1024 * 1024
        ),
    )(
        *(
            pltpu.with_memory_space_constraint(array, pltpu.HBM)
            for array in (
                cube,
                time,
                weight.reshape(1, LOCAL),
                first,
                second.T,
                depth.T,
                owner.reshape(1, FIRST),
            )
        )
    )


def solution(mesh):
    in_specs = (
        P("off", "tile", None, None),
        P("tile", None, None),
        P("off"),
        P("tile", None),
        P(),
        P(),
        P(),
    )
    out_specs = P("tile", "off", None)
    return jax.shard_map(local, mesh=mesh, in_specs=in_specs, out_specs=out_specs, check_vma=False)
```

```python
import jax
import jax.numpy as jnp
from jax import lax
from jax.experimental import pallas as pl
from jax.experimental.pallas import tpu as pltpu
from jax.sharding import PartitionSpec as P

MESH = pl.DeviceIdType.MESH
F32 = jnp.float32
BF16 = jnp.bfloat16
HIGHEST = lax.Precision.HIGHEST

NH = 64
LOCAL = 4
ROWS = 16
HALF = 8
N = 128
COARSE = 16
FIRST = 32
WIDE = FIRST * COARSE
OFFS = 16
GROUP = 16
STRIP = 32
DEVICES = 256
EARLY = (1, 0)
KEEP = 64
PARTS = [(0, 4), (4, 2), (6, 1), (7, 1)]


def iota(shape, axis):
    return lax.broadcasted_iota(jnp.int32, shape, axis)


def dot(a, b):
    return jnp.dot(a, b, preferred_element_type=F32)


def split(x):
    high = x.astype(BF16)
    return high, (x - high.astype(F32)).astype(BF16)


def term(difference, factor):
    last = iota(difference.shape, 1) == N - 1
    following = jnp.where(last, 0.0, pltpu.roll(difference, N - 1, 1))
    return (factor * difference) * (following - difference)


def pick(row, index):
    return jnp.sum(jnp.where(iota(row.shape, 1) == index, row, 0.0), axis=1, keepdims=True)


def hops(size, step):
    return min(step, size - step)


PLANE = sorted(
    [(dx, dy) for dx in range(4) for dy in range(4) if dx or dy],
    key=lambda d: (-hops(4, d[0]) - hops(4, d[1]), d),
)
LINE = sorted(
    [(dz, dc) for dz in range(8) for dc in range(2) if dz or dc],
    key=lambda d: (-hops(8, d[0]) - d[1], d),
)


def kernel(
    cube, time, weight, first, second, depth, owner, out,
    cube_v, time_v, weight_v, first_v, second_v, depth_v, owner_v,
    before, after, rest, weight_before, grad, chosen, place,
    send1, recv1, send2, recv2, direct_row, direct,
    load_sem, up_send, up_recv, down_send, down_recv, word_send, word_recv,
    s1_send, s1_recv, s2_send, s2_recv, near_sem, far_sem, core_sem,
    short_send, short_recv, more_send, more_recv, direct_send, direct_recv, early_sem,
):
    tile = lax.axis_index("tile")
    off = lax.axis_index("off")
    x, z_high, core = lax.div(tile, 4), lax.rem(lax.div(tile, 2), 2), lax.rem(tile, 2)
    z_low, y = lax.div(off, 4), lax.rem(off, 4)
    z = z_high * 4 + z_low
    has_after = off < OFFS - 1
    has_before = off > 0

    tile_x = [lax.rem(x + dx, 4) * 4 for dx in range(4)]
    off_y = [lax.rem(y + dy, 4) for dy in range(4)]
    cores = [core, 1 - core]
    turned = [lax.rem(z + dz, 8) for dz in range(8)]
    tile_z = [lax.div(to_z, 4) * 2 for to_z in turned]
    row_z = [lax.rem(to_z, 4) for to_z in turned]
    rest_tile, rest_off = z_high * 2 + core, z_low * 4
    plane_tile = [tile_x[dx] + rest_tile for dx in range(4)]
    plane_off = [rest_off + off_y[dy] for dy in range(4)]
    line_tile = [[tile_x[0] + tile_z[dz] + cores[dc] for dc in range(2)] for dz in range(8)]
    line_off = [row_z[dz] * 4 + y for dz in range(8)]

    def around(dx=0, dy=0, dz=0, dc=0):
        if dx or dy:
            return plane_tile[dx], plane_off[dy]
        return line_tile[dz][dc], line_off[dz]

    def signal(semaphore, device):
        pl.semaphore_signal(semaphore, inc=1, device_id=device, device_id_type=MESH)

    beside = [dict(dy=1), dict(dy=3), dict(dz=1), dict(dz=7), dict(dx=1), dict(dx=3), dict(dc=1)]
    beyond = [dict(dy=2), dict(dz=2), dict(dz=6), dict(dx=2)]
    barrier = pltpu.get_barrier_semaphore()
    turns_after = jnp.logical_and(y == 3, has_after)
    turns_before = jnp.logical_and(y == 0, has_before)

    @pl.when(turns_after)
    def _():
        signal(barrier, (tile, off + 1))

    @pl.when(turns_before)
    def _():
        signal(barrier, (tile, off - 1))

    for d in beside:
        signal(barrier, around(**d))
    loads = [
        pltpu.make_async_copy(src, dst, load_sem.at[i])
        for i, (src, dst) in enumerate(
            [
                (weight, weight_v),
                (first, first_v),
                (second, second_v),
                (depth, depth_v),
                (owner, owner_v),
                (time, time_v),
                (cube, cube_v),
            ]
        )
    ]
    extra = turns_after.astype(jnp.int32) + turns_before.astype(jnp.int32)
    pl.semaphore_wait(barrier, len(beside) + extra)

    def up(k):
        start, size = PARTS[k]
        return pltpu.make_async_remote_copy(
            src_ref=cube.at[LOCAL - 1, pl.ds(HALF + start, size)],
            dst_ref=before.at[pl.ds(start, size)],
            send_sem=up_send.at[k],
            recv_sem=up_recv.at[k],
            device_id=(tile, off + 1),
            device_id_type=MESH,
        )

    def down(k):
        start, size = PARTS[k]
        return pltpu.make_async_remote_copy(
            src_ref=cube.at[0, pl.ds(start, size)],
            dst_ref=after.at[pl.ds(start, size)],
            send_sem=down_send.at[k],
            recv_sem=down_recv.at[k],
            device_id=(tile, off - 1),
            device_id_type=MESH,
        )

    last = HALF - 1
    short = pltpu.make_async_remote_copy(
        src_ref=cube.at[0, last, pl.ds(0, KEEP)],
        dst_ref=after.at[last, pl.ds(0, KEEP)],
        send_sem=short_send,
        recv_sem=short_recv,
        device_id=(tile, off - 1),
        device_id_type=MESH,
    )
    more = pltpu.make_async_remote_copy(
        src_ref=cube.at[LOCAL - 1, last, pl.ds(KEEP, N - KEEP)],
        dst_ref=rest,
        send_sem=more_send,
        recv_sem=more_recv,
        device_id=(tile, off + 1),
        device_id_type=MESH,
    )
    in_corner = jnp.logical_and(x == 0, y == 0)
    is_early = jnp.logical_and(tile == EARLY[0], off == EARLY[1])
    straight_after = jnp.logical_and(has_after, y < 3)
    straight_before = jnp.logical_and(has_before, y > 0)

    word = pltpu.make_async_remote_copy(
        src_ref=weight,
        dst_ref=weight_before,
        send_sem=word_send,
        recv_sem=word_recv,
        device_id=(tile, off + 1),
        device_id_type=MESH,
    )

    @pl.when(has_after)
    def _():
        word.start()
        for k in range(len(PARTS) - 1):
            up(k).start()

    @pl.when(has_before)
    def _():
        for k in range(len(PARTS) - 1):
            down(k).start()

    @pl.when(turns_after)
    def _():
        more.start()

    @pl.when(has_after)
    def _():
        up(len(PARTS) - 1).start()

    @pl.when(straight_before)
    def _():
        down(len(PARTS) - 1).start()

    @pl.when(turns_before)
    def _():
        short.start()

    for d in beside:
        signal(near_sem, around(**d))
    for load in loads:
        load.start()
    for load in loads[:5]:
        load.wait()

    rows = [second_v[b : b + 1, :] for q in range(4) for b in range(q, COARSE, 4)]
    second_high, second_low = split(jnp.concatenate(rows, axis=0))
    left = jnp.concatenate(
        [
            jnp.concatenate([second_high, second_high], axis=1),
            jnp.concatenate([second_low, jnp.zeros_like(second_low)], axis=1),
        ],
        axis=0,
    )

    unit = (iota((FIRST, WIDE), 0) == iota((FIRST, WIDE), 1) // COARSE).astype(F32)
    owners = jnp.dot(
        jnp.broadcast_to(owner_v[...].astype(F32), (8, FIRST)), unit,
        precision=HIGHEST, preferred_element_type=F32,
    )
    owned = (iota((FIRST, WIDE), 0).astype(F32) == owners[0:1]).astype(F32)
    chosen[...] = jnp.dot(first_v[...], owned, precision=HIGHEST, preferred_element_type=F32)
    depth_wide = jnp.transpose(jnp.concatenate([depth_v[...]] * (N // COARSE), axis=0))

    @pl.loop(0, HALF)
    def _(k):
        for p in range(2):
            row = chosen[pl.ds(p * HALF + k, 1), :]
            for g in range(WIDE // N):
                high, low = split(depth_wide * row[:, g * N : (g + 1) * N])
                place[k, p * N : (p + 1) * N, g * N : (g + 1) * N] = high
                place[k, p * N : (p + 1) * N, WIDE + g * N : WIDE + (g + 1) * N] = low

    pl.semaphore_wait(near_sem, len(beside))
    for d in beyond:
        signal(far_sem, around(**d))

    own = weight_v[...].astype(F32)
    scale = [pick(own * own, h) for h in range(LOCAL)]

    for load in loads[5:]:
        load.wait()

    @pl.loop(0, ROWS)
    def _(r):
        for s in range(0, N, STRIP):
            strip = pl.ds(s, STRIP)
            planes = [cube_v[h, r, strip, :] for h in range(LOCAL)]
            total = term(planes[1] - planes[0], scale[0])
            for h in range(1, LOCAL - 1):
                total += term(planes[h + 1] - planes[h], scale[h])
            grad[r, strip, :] = total
            w = time_v[r, strip, :]
            time_v[r, strip, :] = w * w * (1.0 / NH)

    pl.semaphore_wait(far_sem, len(beyond))
    signal(core_sem, around(dc=1))

    @pl.when(jnp.logical_not(has_after))
    def _():
        @pl.loop(0, HALF)
        def _(k):
            after[k] = jnp.zeros((N, N), F32)
            for s in range(0, N, STRIP):
                strip = pl.ds(s, STRIP)
                grad[HALF + k, strip, :] += term(
                    -cube_v[LOCAL - 1, HALF + k, strip, :], scale[LOCAL - 1]
                )

    @pl.when(jnp.logical_not(has_before))
    def _():
        weight_before[...] = jnp.zeros((1, LOCAL), jnp.int32)

        @pl.loop(0, HALF)
        def _(k):
            before[k] = jnp.zeros((N, N), F32)

    @pl.when(has_before)
    def _():
        word.wait_recv()

    theirs = weight_before[...].astype(F32)
    scale_before = pick(theirs * theirs, LOCAL - 1)

    def step(k, coarse):
        low_rows = time_v[k] * (grad[k] + term(after[k] - cube_v[LOCAL - 1, k], scale[LOCAL - 1]))
        high_rows = time_v[HALF + k] * (
            grad[HALF + k] + term(cube_v[0, HALF + k] - before[k], scale_before)
        )
        a_high, a_low = split(low_rows)
        b_high, b_low = split(high_rows)
        right = jnp.concatenate(
            [
                jnp.concatenate([a_high, b_high], axis=1),
                jnp.concatenate([a_low, b_low], axis=1),
            ],
            axis=0,
        )
        along = dot(left, right)
        along = along[:COARSE] + along[COARSE:]
        both = dot(jnp.concatenate(split(along), axis=0), place[k])
        both = both[:COARSE] + both[COARSE:]
        return coarse + (both[:, :WIDE] + both[:, WIDE:])

    pl.semaphore_wait(core_sem, 1)

    @pl.when(in_corner)
    def _():
        for dx, dy in PLANE:
            signal(early_sem, around(dx=dx, dy=dy))

    @pl.when(jnp.logical_not(in_corner))
    def _():
        pl.semaphore_wait(early_sem, 1)

    coarse = jnp.zeros((COARSE, WIDE), F32)
    for k, (start, size) in enumerate(PARTS):
        if k == len(PARTS) - 1:

            @pl.when(turns_before)
            def _():
                more.wait_recv()
                strip = pl.ds(KEEP, N - KEEP)
                grad[last, strip, :] += term(cube_v[0, last, strip, :] - rest[...], scale_before)

            @pl.when(turns_after)
            def _():
                strip = pl.ds(KEEP, N - KEEP)
                after[last, strip, :] = cube_v[LOCAL - 1, last, strip, :]
                short.wait_recv()

        @pl.when(has_after if k < len(PARTS) - 1 else straight_after)
        def _():
            down(k).wait_recv()

        @pl.when(has_before)
        def _():
            up(k).wait_recv()

        if size > 1:
            coarse = lax.fori_loop(start, start + size, step, coarse)
        else:
            coarse = step(start, coarse)
    direct_row[...] = coarse[0:1, 0:N]
    rank = lax.rem(tile * OFFS + off + DEVICES - (EARLY[0] * OFFS + EARLY[1]), DEVICES)
    straight = pltpu.make_async_remote_copy(
        src_ref=direct_row,
        dst_ref=direct.at[rank],
        send_sem=direct_send,
        recv_sem=direct_recv,
        device_id=EARLY,
        device_id_type=MESH,
    )

    @pl.when(jnp.logical_not(is_early))
    def _():
        straight.start()

    for to_x in range(4):
        for to_y in range(4):
            send1[to_x * 4 + to_y] = coarse[to_y * 4 : to_y * 4 + 4, to_x * N : (to_x + 1) * N]

    def to_plane(dx, dy):
        index = tile_x[dx] + off_y[dy]
        return pltpu.make_async_remote_copy(
            src_ref=send1.at[index],
            dst_ref=recv1.at[dx * 4 + dy],
            send_sem=s1_send,
            recv_sem=s1_recv,
            device_id=around(dx=dx, dy=dy),
            device_id_type=MESH,
        )

    for d in PLANE:
        to_plane(*d).start()
    recv1[0] = send1[x * 4 + y]
    landed = recv1.at[pl.ds(1, GROUP - 1)]
    pltpu.make_async_copy(landed, landed, s1_recv).wait()
    summed = jnp.sum(recv1[...], axis=0)
    for q in range(4):
        send2[q] = summed[q : q + 1]

    def to_line(dz, dc):
        index = row_z[dz]
        return pltpu.make_async_remote_copy(
            src_ref=send2.at[index],
            dst_ref=recv2.at[dz * 2 + dc],
            send_sem=s2_send,
            recv_sem=s2_recv,
            device_id=around(dz=dz, dc=dc),
            device_id_type=MESH,
        )

    in_early_line = jnp.logical_and(in_corner, jnp.logical_not(is_early))
    for dz, dc in LINE:
        early = jnp.logical_and(turned[dz] == 0, cores[dc] == 1)

        @pl.when(jnp.logical_not(jnp.logical_and(in_corner, early)))
        def _():
            to_line(dz, dc).start()

    def finish(rows):
        mine = z_high * 2 + core
        result = pltpu.roll(
            jnp.sum(rows, axis=0), lax.rem(4 - mine, 4) * (2 * COARSE), 1
        )
        for r in range(2):
            out[r] = result[:, r * COARSE : (r + 1) * COARSE]

    @pl.when(is_early)
    def _():
        direct[0] = direct_row[...]
        landed = direct.at[pl.ds(1, DEVICES - 1)]
        pltpu.make_async_copy(landed, landed, direct_recv).wait()
        finish(direct[...])

    @pl.when(jnp.logical_not(is_early))
    def _():
        recv2[0] = send2[z_low]
        landed = recv2.at[pl.ds(1, GROUP - 1)]
        pltpu.make_async_copy(landed, landed, s2_recv).wait()
        finish(recv2[...])
        straight.wait_send()

    left1 = send1.at[pl.ds(0, GROUP - 1)]
    pltpu.make_async_copy(left1, left1, s1_send).wait()

    @pl.when(in_early_line)
    def _():
        left2 = recv2.at[pl.ds(0, GROUP - 2)]
        pltpu.make_async_copy(left2, left2, s2_send).wait()

    @pl.when(jnp.logical_not(in_early_line))
    def _():
        left2 = recv2.at[pl.ds(0, GROUP - 1)]
        pltpu.make_async_copy(left2, left2, s2_send).wait()

    @pl.when(has_after)
    def _():
        word.wait_send()
        for k in range(len(PARTS)):
            up(k).wait_send()

    @pl.when(has_before)
    def _():
        for k in range(len(PARTS) - 1):
            down(k).wait_send()

    @pl.when(straight_before)
    def _():
        down(len(PARTS) - 1).wait_send()

    @pl.when(turns_before)
    def _():
        short.wait_send()

    @pl.when(turns_after)
    def _():
        more.wait_send()


def local(cube, time, weight, first, second, depth, owner):
    hbm = pl.BlockSpec(memory_space=pltpu.HBM)
    dma = pltpu.SemaphoreType.DMA
    return pl.pallas_call(
        kernel,
        out_shape=jax.ShapeDtypeStruct((2, 1, COARSE), F32),
        in_specs=[hbm] * 7,
        out_specs=pl.BlockSpec(memory_space=pltpu.VMEM),
        scratch_shapes=[
            pltpu.VMEM((LOCAL, ROWS, N, N), F32),
            pltpu.VMEM((ROWS, N, N), F32),
            pltpu.VMEM((1, LOCAL), jnp.int32),
            pltpu.VMEM((ROWS, FIRST), F32),
            pltpu.VMEM((COARSE, N), F32),
            pltpu.VMEM((COARSE, N), F32),
            pltpu.VMEM((1, FIRST), jnp.int32),
            pltpu.VMEM((HALF, N, N), F32),
            pltpu.VMEM((HALF, N, N), F32),
            pltpu.VMEM((N - KEEP, N), F32),
            pltpu.VMEM((1, LOCAL), jnp.int32),
            pltpu.VMEM((ROWS, N, N), F32),
            pltpu.VMEM((ROWS, WIDE), F32),
            pltpu.VMEM((HALF, 2 * N, 2 * WIDE), BF16),
            pltpu.VMEM((GROUP, 4, N), F32),
            pltpu.VMEM((GROUP, 4, N), F32),
            pltpu.VMEM((4, 1, N), F32),
            pltpu.VMEM((GROUP, 1, N), F32),
            pltpu.VMEM((1, N), F32),
            pltpu.VMEM((DEVICES, 1, N), F32),
            dma((7,)),
            dma((len(PARTS),)),
            dma((len(PARTS),)),
            dma((len(PARTS),)),
            dma((len(PARTS),)),
            dma,
            dma,
            dma,
            dma,
            dma,
            dma,
            pltpu.SemaphoreType.REGULAR,
            pltpu.SemaphoreType.REGULAR,
            pltpu.SemaphoreType.REGULAR,
            dma,
            dma,
            dma,
            dma,
            dma,
            dma,
            pltpu.SemaphoreType.REGULAR,
        ],
        compiler_params=pltpu.CompilerParams(
            collective_id=0, has_side_effects=True, vmem_limit_bytes=24 * 1024 * 1024
        ),
    )(
        *(
            pltpu.with_memory_space_constraint(array, pltpu.HBM)
            for array in (
                cube,
                time,
                weight.reshape(1, LOCAL),
                first,
                second.T,
                depth.T,
                owner.reshape(1, FIRST),
            )
        )
    )


def solution(mesh):
    in_specs = (
        P("off", "tile", None, None),
        P("tile", None, None),
        P("off"),
        P("tile", None),
        P(),
        P(),
        P(),
    )
    out_specs = P("tile", "off", None)
    return jax.shard_map(local, mesh=mesh, in_specs=in_specs, out_specs=out_specs, check_vma=False)
```

```python
import jax
import jax.numpy as jnp
from jax import lax
from jax.experimental import pallas as pl
from jax.experimental.pallas import tpu as pltpu
from jax.sharding import PartitionSpec as P

MESH = pl.DeviceIdType.MESH
F32 = jnp.float32
BF16 = jnp.bfloat16
HIGHEST = lax.Precision.HIGHEST

NH = 64
LOCAL = 4
ROWS = 16
HALF = 8
N = 128
COARSE = 16
FIRST = 32
WIDE = FIRST * COARSE
OFFS = 16
GROUP = 16
STRIP = 32
DEVICES = 256
EARLY = [
    ((1, 0), 0, 0),
    ((0, 4), 1, 0),
    ((1, 4), 1, 0),
    ((0, 1), 4, 0),
    ((1, 1), 4, 0),
    ((4, 0), 0, 1),
    ((5, 0), 0, 1),
]
EARLY_ROWS = [(0, 0), (1, 0), (4, 0), (0, 1)]
KEEP = 64
PARTS = [(0, 4), (4, 2), (6, 1), (7, 1)]


def iota(shape, axis):
    return lax.broadcasted_iota(jnp.int32, shape, axis)


def dot(a, b):
    return jnp.dot(a, b, preferred_element_type=F32)


def split(x):
    high = x.astype(BF16)
    return high, (x - high.astype(F32)).astype(BF16)


def term(difference, factor):
    last = iota(difference.shape, 1) == N - 1
    following = jnp.where(last, 0.0, pltpu.roll(difference, N - 1, 1))
    return (factor * difference) * (following - difference)


def pick(row, index):
    return jnp.sum(jnp.where(iota(row.shape, 1) == index, row, 0.0), axis=1, keepdims=True)


def total(rows):
    while rows.shape[0] > 1:
        half = rows.shape[0] // 2
        rows = rows[:half] + rows[half:]
    return rows[0]


def hops(size, step):
    return min(step, size - step)


PLANE = sorted(
    [(dx, dy) for dx in range(4) for dy in range(4) if dx or dy],
    key=lambda d: (-hops(4, d[0]) - hops(4, d[1]), d),
)
LINE = sorted(
    [(dz, dc) for dz in range(8) for dc in range(2) if dz or dc],
    key=lambda d: (-hops(8, d[0]) - d[1], d),
)


def kernel(
    cube, time, weight, first, second, depth, owner, out,
    cube_v, time_v, weight_v, first_v, second_v, depth_v, owner_v,
    before, after, rest, weight_before, grad, chosen, place,
    send1, recv1, send2, recv2, direct_row, direct,
    load_sem, up_send, up_recv, down_send, down_recv, word_send, word_recv,
    s1_send, s1_recv, s2_send, s2_recv, near_sem, far_sem, core_sem,
    short_send, short_recv, more_send, more_recv, direct_send, direct_recv, early_sem, root_sem,
):
    tile = lax.axis_index("tile")
    off = lax.axis_index("off")
    x, z_high, core = lax.div(tile, 4), lax.rem(lax.div(tile, 2), 2), lax.rem(tile, 2)
    z_low, y = lax.div(off, 4), lax.rem(off, 4)
    z = z_high * 4 + z_low
    has_after = off < OFFS - 1
    has_before = off > 0

    tile_x = [lax.rem(x + dx, 4) * 4 for dx in range(4)]
    off_y = [lax.rem(y + dy, 4) for dy in range(4)]
    cores = [core, 1 - core]
    turned = [lax.rem(z + dz, 8) for dz in range(8)]
    tile_z = [lax.div(to_z, 4) * 2 for to_z in turned]
    row_z = [lax.rem(to_z, 4) for to_z in turned]
    rest_tile, rest_off = z_high * 2 + core, z_low * 4
    plane_tile = [tile_x[dx] + rest_tile for dx in range(4)]
    plane_off = [rest_off + off_y[dy] for dy in range(4)]
    line_tile = [[tile_x[0] + tile_z[dz] + cores[dc] for dc in range(2)] for dz in range(8)]
    line_off = [row_z[dz] * 4 + y for dz in range(8)]

    def around(dx=0, dy=0, dz=0, dc=0):
        if dx or dy:
            return plane_tile[dx], plane_off[dy]
        return line_tile[dz][dc], line_off[dz]

    def signal(semaphore, device):
        pl.semaphore_signal(semaphore, inc=1, device_id=device, device_id_type=MESH)

    beside = [dict(dy=1), dict(dy=3), dict(dz=1), dict(dz=7), dict(dx=1), dict(dx=3), dict(dc=1)]
    beyond = [dict(dy=2), dict(dz=2), dict(dz=6), dict(dx=2)]
    barrier = pltpu.get_barrier_semaphore()
    turns_after = jnp.logical_and(y == 3, has_after)
    turns_before = jnp.logical_and(y == 0, has_before)

    @pl.when(turns_after)
    def _():
        signal(barrier, (tile, off + 1))

    @pl.when(turns_before)
    def _():
        signal(barrier, (tile, off - 1))

    for d in beside:
        signal(barrier, around(**d))
    loads = [
        pltpu.make_async_copy(src, dst, load_sem.at[i])
        for i, (src, dst) in enumerate(
            [
                (weight, weight_v),
                (first, first_v),
                (second, second_v),
                (depth, depth_v),
                (owner, owner_v),
                (time, time_v),
                (cube, cube_v),
            ]
        )
    ]
    extra = turns_after.astype(jnp.int32) + turns_before.astype(jnp.int32)
    pl.semaphore_wait(barrier, len(beside) + extra)

    def up(k):
        start, size = PARTS[k]
        return pltpu.make_async_remote_copy(
            src_ref=cube.at[LOCAL - 1, pl.ds(HALF + start, size)],
            dst_ref=before.at[pl.ds(start, size)],
            send_sem=up_send.at[k],
            recv_sem=up_recv.at[k],
            device_id=(tile, off + 1),
            device_id_type=MESH,
        )

    def down(k):
        start, size = PARTS[k]
        return pltpu.make_async_remote_copy(
            src_ref=cube.at[0, pl.ds(start, size)],
            dst_ref=after.at[pl.ds(start, size)],
            send_sem=down_send.at[k],
            recv_sem=down_recv.at[k],
            device_id=(tile, off - 1),
            device_id_type=MESH,
        )

    last = HALF - 1
    short = pltpu.make_async_remote_copy(
        src_ref=cube.at[0, last, pl.ds(0, KEEP)],
        dst_ref=after.at[last, pl.ds(0, KEEP)],
        send_sem=short_send,
        recv_sem=short_recv,
        device_id=(tile, off - 1),
        device_id_type=MESH,
    )
    more = pltpu.make_async_remote_copy(
        src_ref=cube.at[LOCAL - 1, last, pl.ds(KEEP, N - KEEP)],
        dst_ref=rest,
        send_sem=more_send,
        recv_sem=more_recv,
        device_id=(tile, off + 1),
        device_id_type=MESH,
    )
    in_corner = jnp.logical_and(x == 0, y == 0)

    def early(total, to_core):
        return jnp.logical_or(total == 1, jnp.logical_and(total == 0, to_core == 1))

    is_early = early(x + y + z, core)
    is_root = jnp.logical_and(in_corner, jnp.logical_and(z == 0, core == 0))
    straight_after = jnp.logical_and(has_after, y < 3)
    straight_before = jnp.logical_and(has_before, y > 0)

    word = pltpu.make_async_remote_copy(
        src_ref=weight,
        dst_ref=weight_before,
        send_sem=word_send,
        recv_sem=word_recv,
        device_id=(tile, off + 1),
        device_id_type=MESH,
    )

    @pl.when(has_after)
    def _():
        word.start()
        for k in range(len(PARTS) - 1):
            up(k).start()

    @pl.when(has_before)
    def _():
        for k in range(len(PARTS) - 1):
            down(k).start()

    @pl.when(turns_after)
    def _():
        more.start()

    @pl.when(has_after)
    def _():
        up(len(PARTS) - 1).start()

    @pl.when(straight_before)
    def _():
        down(len(PARTS) - 1).start()

    @pl.when(turns_before)
    def _():
        short.start()

    for d in beside:
        signal(near_sem, around(**d))
    for load in loads:
        load.start()
    for load in loads[:5]:
        load.wait()

    rows = [second_v[b : b + 1, :] for q in range(4) for b in range(q, COARSE, 4)]
    second_high, second_low = split(jnp.concatenate(rows, axis=0))
    left = jnp.concatenate(
        [
            jnp.concatenate([second_high, second_high], axis=1),
            jnp.concatenate([second_low, jnp.zeros_like(second_low)], axis=1),
        ],
        axis=0,
    )

    unit = (iota((FIRST, WIDE), 0) == iota((FIRST, WIDE), 1) // COARSE).astype(F32)
    owners = jnp.dot(
        jnp.broadcast_to(owner_v[...].astype(F32), (8, FIRST)), unit,
        precision=HIGHEST, preferred_element_type=F32,
    )
    owned = (iota((FIRST, WIDE), 0).astype(F32) == owners[0:1]).astype(F32)
    chosen[...] = jnp.dot(first_v[...], owned, precision=HIGHEST, preferred_element_type=F32)
    depth_wide = jnp.transpose(jnp.concatenate([depth_v[...]] * (N // COARSE), axis=0))

    @pl.loop(0, HALF)
    def _(k):
        for p in range(2):
            row = chosen[pl.ds(p * HALF + k, 1), :]
            for g in range(WIDE // N):
                high, low = split(depth_wide * row[:, g * N : (g + 1) * N])
                place[k, p * N : (p + 1) * N, g * N : (g + 1) * N] = high
                place[k, p * N : (p + 1) * N, WIDE + g * N : WIDE + (g + 1) * N] = low

    pl.semaphore_wait(near_sem, len(beside))
    for d in beyond:
        signal(far_sem, around(**d))

    own = weight_v[...].astype(F32)
    scale = [pick(own * own, h) for h in range(LOCAL)]

    for load in loads[5:]:
        load.wait()

    @pl.loop(0, ROWS)
    def _(r):
        for s in range(0, N, STRIP):
            strip = pl.ds(s, STRIP)
            planes = [cube_v[h, r, strip, :] for h in range(LOCAL)]
            total = term(planes[1] - planes[0], scale[0])
            for h in range(1, LOCAL - 1):
                total += term(planes[h + 1] - planes[h], scale[h])
            grad[r, strip, :] = total
            w = time_v[r, strip, :]
            time_v[r, strip, :] = w * w * (1.0 / NH)

    pl.semaphore_wait(far_sem, len(beyond))
    signal(core_sem, around(dc=1))

    @pl.when(jnp.logical_not(has_after))
    def _():
        @pl.loop(0, HALF)
        def _(k):
            after[k] = jnp.zeros((N, N), F32)
            for s in range(0, N, STRIP):
                strip = pl.ds(s, STRIP)
                grad[HALF + k, strip, :] += term(
                    -cube_v[LOCAL - 1, HALF + k, strip, :], scale[LOCAL - 1]
                )

    @pl.when(jnp.logical_not(has_before))
    def _():
        weight_before[...] = jnp.zeros((1, LOCAL), jnp.int32)

        @pl.loop(0, HALF)
        def _(k):
            before[k] = jnp.zeros((N, N), F32)

    @pl.when(has_before)
    def _():
        word.wait_recv()

    theirs = weight_before[...].astype(F32)
    scale_before = pick(theirs * theirs, LOCAL - 1)

    def step(k, coarse):
        low_rows = time_v[k] * (grad[k] + term(after[k] - cube_v[LOCAL - 1, k], scale[LOCAL - 1]))
        high_rows = time_v[HALF + k] * (
            grad[HALF + k] + term(cube_v[0, HALF + k] - before[k], scale_before)
        )
        a_high, a_low = split(low_rows)
        b_high, b_low = split(high_rows)
        right = jnp.concatenate(
            [
                jnp.concatenate([a_high, b_high], axis=1),
                jnp.concatenate([a_low, b_low], axis=1),
            ],
            axis=0,
        )
        along = dot(left, right)
        along = along[:COARSE] + along[COARSE:]
        both = dot(jnp.concatenate(split(along), axis=0), place[k])
        both = both[:COARSE] + both[COARSE:]
        return coarse + (both[:, :WIDE] + both[:, WIDE:])

    pl.semaphore_wait(core_sem, 1)

    @pl.when(is_root)
    def _():
        for dz, dc in LINE:
            signal(root_sem, around(dz=dz, dc=dc))

    @pl.when(jnp.logical_and(in_corner, jnp.logical_not(is_root)))
    def _():
        pl.semaphore_wait(root_sem, 1)

    @pl.when(in_corner)
    def _():
        for dx, dy in PLANE:
            signal(early_sem, around(dx=dx, dy=dy))

    @pl.when(jnp.logical_not(in_corner))
    def _():
        pl.semaphore_wait(early_sem, 1)

    coarse = jnp.zeros((COARSE, WIDE), F32)
    for k, (start, size) in enumerate(PARTS):
        if k == len(PARTS) - 1:

            @pl.when(turns_before)
            def _():
                more.wait_recv()
                strip = pl.ds(KEEP, N - KEEP)
                grad[last, strip, :] += term(cube_v[0, last, strip, :] - rest[...], scale_before)

            @pl.when(turns_after)
            def _():
                strip = pl.ds(KEEP, N - KEEP)
                after[last, strip, :] = cube_v[LOCAL - 1, last, strip, :]
                short.wait_recv()

        @pl.when(has_after if k < len(PARTS) - 1 else straight_after)
        def _():
            down(k).wait_recv()

        @pl.when(has_before)
        def _():
            up(k).wait_recv()

        if size > 1:
            coarse = lax.fori_loop(start, start + size, step, coarse)
        else:
            coarse = step(start, coarse)
    for i, (row, block) in enumerate(EARLY_ROWS):
        direct_row[i] = coarse[row : row + 1, block * N : (block + 1) * N]

    def start_straight(target, row, block):
        to_tile, to_off = target
        me = tile * OFFS + off
        there = to_tile * OFFS + to_off

        @pl.when(me != there)
        def _():
            pltpu.make_async_remote_copy(
                src_ref=direct_row.at[EARLY_ROWS.index((row, block))],
                dst_ref=direct.at[lax.rem(me + DEVICES - there, DEVICES)],
                send_sem=direct_send,
                recv_sem=direct_recv,
                device_id=target,
                device_id_type=MESH,
            ).start()

    start_straight(*EARLY[0])
    for to_x in range(4):
        for to_y in range(4):
            send1[to_x * 4 + to_y] = coarse[to_y * 4 : to_y * 4 + 4, to_x * N : (to_x + 1) * N]

    def to_plane(dx, dy):
        index = tile_x[dx] + off_y[dy]
        return pltpu.make_async_remote_copy(
            src_ref=send1.at[index],
            dst_ref=recv1.at[dx * 4 + dy],
            send_sem=s1_send,
            recv_sem=s1_recv,
            device_id=around(dx=dx, dy=dy),
            device_id_type=MESH,
        )

    for d in PLANE:
        to_plane(*d).start()

    for target in EARLY[1:]:
        start_straight(*target)

    @pl.when(has_after)
    def _():
        word.wait_send()
        for k in range(len(PARTS)):
            up(k).wait_send()

    @pl.when(has_before)
    def _():
        for k in range(len(PARTS) - 1):
            down(k).wait_send()

    @pl.when(straight_before)
    def _():
        down(len(PARTS) - 1).wait_send()

    @pl.when(turns_before)
    def _():
        short.wait_send()

    @pl.when(turns_after)
    def _():
        more.wait_send()

    recv1[0] = send1[x * 4 + y]
    landed = recv1.at[pl.ds(1, GROUP - 1)]
    pltpu.make_async_copy(landed, landed, s1_recv).wait()
    summed = total(recv1[...])
    for q in range(4):
        send2[q] = summed[q : q + 1]

    def to_line(dz, dc):
        index = row_z[dz]
        return pltpu.make_async_remote_copy(
            src_ref=send2.at[index],
            dst_ref=recv2.at[dz * 2 + dc],
            send_sem=s2_send.at[dz * 2 + dc],
            recv_sem=s2_recv,
            device_id=around(dz=dz, dc=dc),
            device_id_type=MESH,
        )

    takes_part = {
        (dz, dc): jnp.logical_not(early(x + y + turned[dz], cores[dc])) for dz, dc in LINE
    }
    for d in LINE:

        @pl.when(takes_part[d])
        def _():
            to_line(*d).start()

    left1 = send1.at[pl.ds(0, GROUP - 1)]
    pltpu.make_async_copy(left1, left1, s1_send).wait()

    def finish(rows):
        mine = z_high * 2 + core
        result = pltpu.roll(
            total(rows), lax.rem(4 - mine, 4) * (2 * COARSE), 1
        )
        for r in range(2):
            out[r] = result[:, r * COARSE : (r + 1) * COARSE]

    for d in LINE:

        @pl.when(takes_part[d])
        def _():
            to_line(*d).wait_send()

    @pl.when(is_early)
    def _():
        for i, (row, block) in enumerate(EARLY_ROWS):
            yours = jnp.logical_and(
                x == block, jnp.logical_and(y == row // 4, z_low == row % 4)
            )

            @pl.when(yours)
            def _():
                direct[0] = direct_row[i]

        landed = direct.at[pl.ds(1, DEVICES - 1)]
        pltpu.make_async_copy(landed, landed, direct_recv).wait()
        finish(direct[...])
        gone = direct.at[pl.ds(0, len(EARLY) - 1)]
        pltpu.make_async_copy(gone, gone, direct_send).wait()

    @pl.when(jnp.logical_not(is_early))
    def _():
        recv2[0] = send2[z_low]
        landed = recv2.at[pl.ds(1, GROUP - 1)]
        pltpu.make_async_copy(landed, landed, s2_recv).wait()
        finish(recv2[...])
        gone = direct.at[pl.ds(0, len(EARLY))]
        pltpu.make_async_copy(gone, gone, direct_send).wait()

def local(cube, time, weight, first, second, depth, owner):
    hbm = pl.BlockSpec(memory_space=pltpu.HBM)
    dma = pltpu.SemaphoreType.DMA
    return pl.pallas_call(
        kernel,
        out_shape=jax.ShapeDtypeStruct((2, 1, COARSE), F32),
        in_specs=[hbm] * 7,
        out_specs=pl.BlockSpec(memory_space=pltpu.VMEM),
        scratch_shapes=[
            pltpu.VMEM((LOCAL, ROWS, N, N), F32),
            pltpu.VMEM((ROWS, N, N), F32),
            pltpu.VMEM((1, LOCAL), jnp.int32),
            pltpu.VMEM((ROWS, FIRST), F32),
            pltpu.VMEM((COARSE, N), F32),
            pltpu.VMEM((COARSE, N), F32),
            pltpu.VMEM((1, FIRST), jnp.int32),
            pltpu.VMEM((HALF, N, N), F32),
            pltpu.VMEM((HALF, N, N), F32),
            pltpu.VMEM((N - KEEP, N), F32),
            pltpu.VMEM((1, LOCAL), jnp.int32),
            pltpu.VMEM((ROWS, N, N), F32),
            pltpu.VMEM((ROWS, WIDE), F32),
            pltpu.VMEM((HALF, 2 * N, 2 * WIDE), BF16),
            pltpu.VMEM((GROUP, 4, N), F32),
            pltpu.VMEM((GROUP, 4, N), F32),
            pltpu.VMEM((4, 1, N), F32),
            pltpu.VMEM((GROUP, 1, N), F32),
            pltpu.VMEM((len(EARLY_ROWS), 1, N), F32),
            pltpu.VMEM((DEVICES, 1, N), F32),
            dma((7,)),
            dma((len(PARTS),)),
            dma((len(PARTS),)),
            dma((len(PARTS),)),
            dma((len(PARTS),)),
            dma,
            dma,
            dma,
            dma,
            dma((GROUP,)),
            dma,
            pltpu.SemaphoreType.REGULAR,
            pltpu.SemaphoreType.REGULAR,
            pltpu.SemaphoreType.REGULAR,
            dma,
            dma,
            dma,
            dma,
            dma,
            dma,
            pltpu.SemaphoreType.REGULAR,
            pltpu.SemaphoreType.REGULAR,
        ],
        compiler_params=pltpu.CompilerParams(
            collective_id=0, has_side_effects=True, vmem_limit_bytes=24 * 1024 * 1024
        ),
    )(
        *(
            pltpu.with_memory_space_constraint(array, pltpu.HBM)
            for array in (
                cube,
                time,
                weight.reshape(1, LOCAL),
                first,
                second.T,
                depth.T,
                owner.reshape(1, FIRST),
            )
        )
    )


def solution(mesh):
    in_specs = (
        P("off", "tile", None, None),
        P("tile", None, None),
        P("off"),
        P("tile", None),
        P(),
        P(),
        P(),
    )
    out_specs = P("tile", "off", None)
    return jax.shard_map(local, mesh=mesh, in_specs=in_specs, out_specs=out_specs, check_vma=False)
```

```python
import jax
import jax.numpy as jnp
from jax import lax
from jax.experimental import pallas as pl
from jax.experimental.pallas import tpu as pltpu
from jax.sharding import PartitionSpec as P

MESH = pl.DeviceIdType.MESH
F32 = jnp.float32
BF16 = jnp.bfloat16
HIGHEST = lax.Precision.HIGHEST

NH = 64
LOCAL = 4
ROWS = 16
HALF = 8
N = 128
COARSE = 16
FIRST = 32
WIDE = FIRST * COARSE
OFFS = 16
GROUP = 16
STRIP = 32
DEVICES = 256
EARLY = [
    ((1, 0), 0, 0),
    ((0, 4), 1, 0),
    ((1, 4), 1, 0),
    ((0, 1), 4, 0),
    ((1, 1), 4, 0),
    ((4, 0), 0, 1),
    ((5, 0), 0, 1),
]
EARLY_ROWS = [(0, 0), (1, 0), (4, 0), (0, 1)]
KEEP = 64
PARTS = [(0, 3), (3, 2), (5, 1), (6, 1), (7, 1)]


def iota(shape, axis):
    return lax.broadcasted_iota(jnp.int32, shape, axis)


def dot(a, b):
    return jnp.dot(a, b, preferred_element_type=F32)


def split(x):
    high = x.astype(BF16)
    return high, (x - high.astype(F32)).astype(BF16)


def term(difference, factor):
    last = iota(difference.shape, 1) == N - 1
    following = jnp.where(last, 0.0, pltpu.roll(difference, N - 1, 1))
    return (factor * difference) * (following - difference)


def pick(row, index):
    return jnp.sum(jnp.where(iota(row.shape, 1) == index, row, 0.0), axis=1, keepdims=True)


def total(rows):
    while rows.shape[0] > 1:
        half = rows.shape[0] // 2
        rows = rows[:half] + rows[half:]
    return rows[0]


def hops(size, step):
    return min(step, size - step)


PLANE = sorted(
    [(dx, dy) for dx in range(4) for dy in range(4) if dx or dy],
    key=lambda d: (-hops(4, d[0]) - hops(4, d[1]), d),
)
LINE = sorted(
    [(dz, dc) for dz in range(8) for dc in range(2) if dz or dc],
    key=lambda d: (-hops(8, d[0]) - d[1], d),
)


def kernel(
    cube, time, weight, first, second, depth, owner, out,
    cube_v, time_v, weight_v, first_v, second_v, depth_v, owner_v,
    before, after, rest, weight_before, grad, chosen, place,
    send1, recv1, send2, recv2, direct_row, direct,
    load_sem, up_send, up_recv, down_send, down_recv, word_send, word_recv,
    s1_send, s1_recv, s2_send, s2_recv, near_sem, far_sem, core_sem,
    short_send, short_recv, more_send, more_recv, direct_send, direct_recv, early_sem, root_sem,
):
    tile = lax.axis_index("tile")
    off = lax.axis_index("off")
    x, z_high, core = lax.div(tile, 4), lax.rem(lax.div(tile, 2), 2), lax.rem(tile, 2)
    z_low, y = lax.div(off, 4), lax.rem(off, 4)
    z = z_high * 4 + z_low
    has_after = off < OFFS - 1
    has_before = off > 0

    tile_x = [lax.rem(x + dx, 4) * 4 for dx in range(4)]
    off_y = [lax.rem(y + dy, 4) for dy in range(4)]
    cores = [core, 1 - core]
    turned = [lax.rem(z + dz, 8) for dz in range(8)]
    tile_z = [lax.div(to_z, 4) * 2 for to_z in turned]
    row_z = [lax.rem(to_z, 4) for to_z in turned]
    rest_tile, rest_off = z_high * 2 + core, z_low * 4
    plane_tile = [tile_x[dx] + rest_tile for dx in range(4)]
    plane_off = [rest_off + off_y[dy] for dy in range(4)]
    line_tile = [[tile_x[0] + tile_z[dz] + cores[dc] for dc in range(2)] for dz in range(8)]
    line_off = [row_z[dz] * 4 + y for dz in range(8)]

    def around(dx=0, dy=0, dz=0, dc=0):
        if dx or dy:
            return plane_tile[dx], plane_off[dy]
        return line_tile[dz][dc], line_off[dz]

    def signal(semaphore, device):
        pl.semaphore_signal(semaphore, inc=1, device_id=device, device_id_type=MESH)

    beside = [dict(dy=1), dict(dy=3), dict(dz=1), dict(dz=7), dict(dx=1), dict(dx=3), dict(dc=1)]
    beyond = [dict(dy=2), dict(dz=2), dict(dz=6), dict(dx=2)]
    barrier = pltpu.get_barrier_semaphore()
    turns_after = jnp.logical_and(y == 3, has_after)
    turns_before = jnp.logical_and(y == 0, has_before)

    @pl.when(turns_after)
    def _():
        signal(barrier, (tile, off + 1))

    @pl.when(turns_before)
    def _():
        signal(barrier, (tile, off - 1))

    for d in beside:
        signal(barrier, around(**d))
    loads = [
        pltpu.make_async_copy(src, dst, load_sem.at[i])
        for i, (src, dst) in enumerate(
            [
                (weight, weight_v),
                (first, first_v),
                (second, second_v),
                (depth, depth_v),
                (owner, owner_v),
                (time, time_v),
                (cube, cube_v),
            ]
        )
    ]
    extra = turns_after.astype(jnp.int32) + turns_before.astype(jnp.int32)
    pl.semaphore_wait(barrier, len(beside) + extra)

    def up(k):
        start, size = PARTS[k]
        return pltpu.make_async_remote_copy(
            src_ref=cube.at[LOCAL - 1, pl.ds(HALF + start, size)],
            dst_ref=before.at[pl.ds(start, size)],
            send_sem=up_send.at[k],
            recv_sem=up_recv.at[k],
            device_id=(tile, off + 1),
            device_id_type=MESH,
        )

    def down(k):
        start, size = PARTS[k]
        return pltpu.make_async_remote_copy(
            src_ref=cube.at[0, pl.ds(start, size)],
            dst_ref=after.at[pl.ds(start, size)],
            send_sem=down_send.at[k],
            recv_sem=down_recv.at[k],
            device_id=(tile, off - 1),
            device_id_type=MESH,
        )

    last = HALF - 1
    short = pltpu.make_async_remote_copy(
        src_ref=cube.at[0, last, pl.ds(0, KEEP)],
        dst_ref=after.at[last, pl.ds(0, KEEP)],
        send_sem=short_send,
        recv_sem=short_recv,
        device_id=(tile, off - 1),
        device_id_type=MESH,
    )
    more = pltpu.make_async_remote_copy(
        src_ref=cube.at[LOCAL - 1, last, pl.ds(KEEP, N - KEEP)],
        dst_ref=rest,
        send_sem=more_send,
        recv_sem=more_recv,
        device_id=(tile, off + 1),
        device_id_type=MESH,
    )
    in_corner = jnp.logical_and(x == 0, y == 0)

    def early(total, to_core):
        return jnp.logical_or(total == 1, jnp.logical_and(total == 0, to_core == 1))

    is_early = early(x + y + z, core)
    is_root = jnp.logical_and(in_corner, jnp.logical_and(z == 0, core == 0))
    straight_after = jnp.logical_and(has_after, y < 3)
    straight_before = jnp.logical_and(has_before, y > 0)

    word = pltpu.make_async_remote_copy(
        src_ref=weight,
        dst_ref=weight_before,
        send_sem=word_send,
        recv_sem=word_recv,
        device_id=(tile, off + 1),
        device_id_type=MESH,
    )

    @pl.when(has_after)
    def _():
        word.start()
        for k in range(len(PARTS) - 1):
            up(k).start()

    @pl.when(has_before)
    def _():
        for k in range(len(PARTS) - 1):
            down(k).start()

    @pl.when(turns_after)
    def _():
        more.start()

    @pl.when(has_after)
    def _():
        up(len(PARTS) - 1).start()

    @pl.when(straight_before)
    def _():
        down(len(PARTS) - 1).start()

    @pl.when(turns_before)
    def _():
        short.start()

    for d in beside:
        signal(near_sem, around(**d))
    for load in loads:
        load.start()
    for load in loads[:5]:
        load.wait()

    rows = [second_v[b : b + 1, :] for q in range(4) for b in range(q, COARSE, 4)]
    second_high, second_low = split(jnp.concatenate(rows, axis=0))
    left = jnp.concatenate(
        [
            jnp.concatenate([second_high, second_high], axis=1),
            jnp.concatenate([second_low, jnp.zeros_like(second_low)], axis=1),
        ],
        axis=0,
    )

    unit = (iota((FIRST, WIDE), 0) == iota((FIRST, WIDE), 1) // COARSE).astype(F32)
    owners = jnp.dot(
        jnp.broadcast_to(owner_v[...].astype(F32), (8, FIRST)), unit,
        precision=HIGHEST, preferred_element_type=F32,
    )
    owned = (iota((FIRST, WIDE), 0).astype(F32) == owners[0:1]).astype(F32)
    chosen[...] = jnp.dot(first_v[...], owned, precision=HIGHEST, preferred_element_type=F32)
    depth_wide = jnp.transpose(jnp.concatenate([depth_v[...]] * (N // COARSE), axis=0))

    @pl.loop(0, HALF)
    def _(k):
        for p in range(2):
            row = chosen[pl.ds(p * HALF + k, 1), :]
            for g in range(WIDE // N):
                high, low = split(depth_wide * row[:, g * N : (g + 1) * N])
                place[k, p * N : (p + 1) * N, g * N : (g + 1) * N] = high
                place[k, p * N : (p + 1) * N, WIDE + g * N : WIDE + (g + 1) * N] = low

    pl.semaphore_wait(near_sem, len(beside))
    for d in beyond:
        signal(far_sem, around(**d))

    own = weight_v[...].astype(F32)
    scale = [pick(own * own, h) for h in range(LOCAL)]

    for load in loads[5:]:
        load.wait()

    @pl.loop(0, ROWS)
    def _(r):
        for s in range(0, N, STRIP):
            strip = pl.ds(s, STRIP)
            planes = [cube_v[h, r, strip, :] for h in range(LOCAL)]
            total = term(planes[1] - planes[0], scale[0])
            for h in range(1, LOCAL - 1):
                total += term(planes[h + 1] - planes[h], scale[h])
            grad[r, strip, :] = total
            w = time_v[r, strip, :]
            time_v[r, strip, :] = w * w * (1.0 / NH)

    pl.semaphore_wait(far_sem, len(beyond))
    signal(core_sem, around(dc=1))

    @pl.when(jnp.logical_not(has_after))
    def _():
        @pl.loop(0, HALF)
        def _(k):
            after[k] = jnp.zeros((N, N), F32)
            for s in range(0, N, STRIP):
                strip = pl.ds(s, STRIP)
                grad[HALF + k, strip, :] += term(
                    -cube_v[LOCAL - 1, HALF + k, strip, :], scale[LOCAL - 1]
                )

    @pl.when(jnp.logical_not(has_before))
    def _():
        weight_before[...] = jnp.zeros((1, LOCAL), jnp.int32)

        @pl.loop(0, HALF)
        def _(k):
            before[k] = jnp.zeros((N, N), F32)

    @pl.when(has_before)
    def _():
        word.wait_recv()

    theirs = weight_before[...].astype(F32)
    scale_before = pick(theirs * theirs, LOCAL - 1)

    def step(k, coarse):
        low_rows = time_v[k] * (grad[k] + term(after[k] - cube_v[LOCAL - 1, k], scale[LOCAL - 1]))
        high_rows = time_v[HALF + k] * (
            grad[HALF + k] + term(cube_v[0, HALF + k] - before[k], scale_before)
        )
        a_high, a_low = split(low_rows)
        b_high, b_low = split(high_rows)
        right = jnp.concatenate(
            [
                jnp.concatenate([a_high, b_high], axis=1),
                jnp.concatenate([a_low, b_low], axis=1),
            ],
            axis=0,
        )
        along = dot(left, right)
        along = along[:COARSE] + along[COARSE:]
        both = dot(jnp.concatenate(split(along), axis=0), place[k])
        both = both[:COARSE] + both[COARSE:]
        return coarse + (both[:, :WIDE] + both[:, WIDE:])

    pl.semaphore_wait(core_sem, 1)

    @pl.when(is_root)
    def _():
        for dz, dc in LINE:
            signal(root_sem, around(dz=dz, dc=dc))

    @pl.when(jnp.logical_and(in_corner, jnp.logical_not(is_root)))
    def _():
        pl.semaphore_wait(root_sem, 1)

    @pl.when(in_corner)
    def _():
        for dx, dy in PLANE:
            signal(early_sem, around(dx=dx, dy=dy))

    @pl.when(jnp.logical_not(in_corner))
    def _():
        pl.semaphore_wait(early_sem, 1)

    coarse = jnp.zeros((COARSE, WIDE), F32)
    for k, (start, size) in enumerate(PARTS):
        if k == len(PARTS) - 1:

            @pl.when(turns_before)
            def _():
                more.wait_recv()
                strip = pl.ds(KEEP, N - KEEP)
                grad[last, strip, :] += term(cube_v[0, last, strip, :] - rest[...], scale_before)

            @pl.when(turns_after)
            def _():
                strip = pl.ds(KEEP, N - KEEP)
                after[last, strip, :] = cube_v[LOCAL - 1, last, strip, :]
                short.wait_recv()

        @pl.when(has_after if k < len(PARTS) - 1 else straight_after)
        def _():
            down(k).wait_recv()

        @pl.when(has_before)
        def _():
            up(k).wait_recv()

        if size > 1:
            coarse = lax.fori_loop(start, start + size, step, coarse)
        else:
            coarse = step(start, coarse)
    for i, (row, block) in enumerate(EARLY_ROWS):
        direct_row[i] = coarse[row : row + 1, block * N : (block + 1) * N]

    def start_straight(target, row, block):
        to_tile, to_off = target
        me = tile * OFFS + off
        there = to_tile * OFFS + to_off

        @pl.when(me != there)
        def _():
            pltpu.make_async_remote_copy(
                src_ref=direct_row.at[EARLY_ROWS.index((row, block))],
                dst_ref=direct.at[lax.rem(me + DEVICES - there, DEVICES)],
                send_sem=direct_send,
                recv_sem=direct_recv,
                device_id=target,
                device_id_type=MESH,
            ).start()

    start_straight(*EARLY[0])
    for to_x in range(4):
        for to_y in range(4):
            send1[to_x * 4 + to_y] = coarse[to_y * 4 : to_y * 4 + 4, to_x * N : (to_x + 1) * N]

    def to_plane(dx, dy):
        index = tile_x[dx] + off_y[dy]
        return pltpu.make_async_remote_copy(
            src_ref=send1.at[index],
            dst_ref=recv1.at[dx * 4 + dy],
            send_sem=s1_send,
            recv_sem=s1_recv,
            device_id=around(dx=dx, dy=dy),
            device_id_type=MESH,
        )

    for d in PLANE:
        to_plane(*d).start()

    for target in EARLY[1:]:
        start_straight(*target)

    @pl.when(has_after)
    def _():
        word.wait_send()
        for k in range(len(PARTS)):
            up(k).wait_send()

    @pl.when(has_before)
    def _():
        for k in range(len(PARTS) - 1):
            down(k).wait_send()

    @pl.when(straight_before)
    def _():
        down(len(PARTS) - 1).wait_send()

    @pl.when(turns_before)
    def _():
        short.wait_send()

    @pl.when(turns_after)
    def _():
        more.wait_send()

    recv1[0] = send1[x * 4 + y]
    landed = recv1.at[pl.ds(1, GROUP - 1)]
    pltpu.make_async_copy(landed, landed, s1_recv).wait()
    summed = total(recv1[...])
    for q in range(4):
        send2[q] = summed[q : q + 1]

    def to_line(dz, dc):
        index = row_z[dz]
        return pltpu.make_async_remote_copy(
            src_ref=send2.at[index],
            dst_ref=recv2.at[dz * 2 + dc],
            send_sem=s2_send.at[dz * 2 + dc],
            recv_sem=s2_recv,
            device_id=around(dz=dz, dc=dc),
            device_id_type=MESH,
        )

    takes_part = {
        (dz, dc): jnp.logical_not(early(x + y + turned[dz], cores[dc])) for dz, dc in LINE
    }
    for d in LINE:

        @pl.when(takes_part[d])
        def _():
            to_line(*d).start()

    left1 = send1.at[pl.ds(0, GROUP - 1)]
    pltpu.make_async_copy(left1, left1, s1_send).wait()

    def finish(rows):
        mine = z_high * 2 + core
        result = pltpu.roll(
            total(rows), lax.rem(4 - mine, 4) * (2 * COARSE), 1
        )
        for r in range(2):
            out[r] = result[:, r * COARSE : (r + 1) * COARSE]

    for d in LINE:

        @pl.when(takes_part[d])
        def _():
            to_line(*d).wait_send()

    @pl.when(is_early)
    def _():
        for i, (row, block) in enumerate(EARLY_ROWS):
            yours = jnp.logical_and(
                x == block, jnp.logical_and(y == row // 4, z_low == row % 4)
            )

            @pl.when(yours)
            def _():
                direct[0] = direct_row[i]

        landed = direct.at[pl.ds(1, DEVICES - 1)]
        pltpu.make_async_copy(landed, landed, direct_recv).wait()
        finish(direct[...])
        gone = direct.at[pl.ds(0, len(EARLY) - 1)]
        pltpu.make_async_copy(gone, gone, direct_send).wait()

    @pl.when(jnp.logical_not(is_early))
    def _():
        recv2[0] = send2[z_low]
        landed = recv2.at[pl.ds(1, GROUP - 1)]
        pltpu.make_async_copy(landed, landed, s2_recv).wait()
        finish(recv2[...])
        gone = direct.at[pl.ds(0, len(EARLY))]
        pltpu.make_async_copy(gone, gone, direct_send).wait()

def local(cube, time, weight, first, second, depth, owner):
    hbm = pl.BlockSpec(memory_space=pltpu.HBM)
    dma = pltpu.SemaphoreType.DMA
    return pl.pallas_call(
        kernel,
        out_shape=jax.ShapeDtypeStruct((2, 1, COARSE), F32),
        in_specs=[hbm] * 7,
        out_specs=pl.BlockSpec(memory_space=pltpu.VMEM),
        scratch_shapes=[
            pltpu.VMEM((LOCAL, ROWS, N, N), F32),
            pltpu.VMEM((ROWS, N, N), F32),
            pltpu.VMEM((1, LOCAL), jnp.int32),
            pltpu.VMEM((ROWS, FIRST), F32),
            pltpu.VMEM((COARSE, N), F32),
            pltpu.VMEM((COARSE, N), F32),
            pltpu.VMEM((1, FIRST), jnp.int32),
            pltpu.VMEM((HALF, N, N), F32),
            pltpu.VMEM((HALF, N, N), F32),
            pltpu.VMEM((N - KEEP, N), F32),
            pltpu.VMEM((1, LOCAL), jnp.int32),
            pltpu.VMEM((ROWS, N, N), F32),
            pltpu.VMEM((ROWS, WIDE), F32),
            pltpu.VMEM((HALF, 2 * N, 2 * WIDE), BF16),
            pltpu.VMEM((GROUP, 4, N), F32),
            pltpu.VMEM((GROUP, 4, N), F32),
            pltpu.VMEM((4, 1, N), F32),
            pltpu.VMEM((GROUP, 1, N), F32),
            pltpu.VMEM((len(EARLY_ROWS), 1, N), F32),
            pltpu.VMEM((DEVICES, 1, N), F32),
            dma((7,)),
            dma((len(PARTS),)),
            dma((len(PARTS),)),
            dma((len(PARTS),)),
            dma((len(PARTS),)),
            dma,
            dma,
            dma,
            dma,
            dma((GROUP,)),
            dma,
            pltpu.SemaphoreType.REGULAR,
            pltpu.SemaphoreType.REGULAR,
            pltpu.SemaphoreType.REGULAR,
            dma,
            dma,
            dma,
            dma,
            dma,
            dma,
            pltpu.SemaphoreType.REGULAR,
            pltpu.SemaphoreType.REGULAR,
        ],
        compiler_params=pltpu.CompilerParams(
            collective_id=0, has_side_effects=True, vmem_limit_bytes=24 * 1024 * 1024
        ),
    )(
        *(
            pltpu.with_memory_space_constraint(array, pltpu.HBM)
            for array in (
                cube,
                time,
                weight.reshape(1, LOCAL),
                first,
                second.T,
                depth.T,
                owner.reshape(1, FIRST),
            )
        )
    )


def solution(mesh):
    in_specs = (
        P("off", "tile", None, None),
        P("tile", None, None),
        P("off"),
        P("tile", None),
        P(),
        P(),
        P(),
    )
    out_specs = P("tile", "off", None)
    return jax.shard_map(local, mesh=mesh, in_specs=in_specs, out_specs=out_specs, check_vma=False)
```
